128 devices in a mesh: row: 16 (over x, y), col: 8 (over z, core).
Axes of the slice: x: 4, y: 4, z: 4, core: 2. Of those that a mesh axis runs over, the one named last changes fastest.
Arguments:
- source_points: bfloat16 [65536, 1024], P('row'), may hold values from -8 to 8
- target_points: bfloat16 [32768, 1024], P('col', 'row'), may hold values from -8 to 8
- source_mass: float32 [65536], P('row'), may hold values from 0.25 to 4
- target_mass: float32 [32768], P('col'), may hold values from 0.25 to 4
- tile_index: int32 [256, 16], P('row', 'col'), may hold values from 0 to 15, as said below
- tile_count: int32 [256, 8], P('row', 'col'), may hold values from 1 to 2, as said below
Outputs:
- source_potential: float32 [65536], P('row')
- target_potential: float32 [32768], P('col')
The draws below stay inside these ranges and needn't reach their ends.
Inputs may be any that keep to these rules, and one draw needn't show every extreme that they name: `tile_index`: within the 2 slots of one source tile and one index of col the target tiles are distinct; every target tile is named by a live slot of some source tile. `tile_count`: each index of row holds, for every index of col, a source tile with all 2 slots live.
All inputs are finite; a program needn't handle non-finite values.
Results may differ from the reference program's by a relative error of at most 0.0003.
Values may be sent and summed in bfloat16 or wider, within the bound.
A program may use at most 128 MiB of HBM per device.

```python
import math
import jax
import jax.numpy as jnp
from jax import lax

D = 1024
TILE = 256
KL = 2
ITERS = 3
SR = 4096
TC = 4096
NS = 65536
NT = 32768
RT = 256
CTL = 16
N_COL = 8


def common_direction(key):
    flips = jax.random.bernoulli(jax.random.fold_in(key, 7), 0.5, (D,))
    return jnp.where(flips, 1.0, -1.0).astype(jnp.float32)


def strong_rows(key, base, count, salt):
    chosen = jax.random.bernoulli(jax.random.fold_in(key, salt), 0.125, (count, 1))
    level = jax.random.uniform(jax.random.fold_in(key, salt + 1), (count, 1), jnp.float32, 60.0, 300.0)
    flips = jax.random.bernoulli(jax.random.fold_in(key, salt + 2), 0.5, (count, 1))
    sign = jnp.where(flips, 1.0, -1.0).astype(jnp.float32)
    magnitude = sign * jnp.sqrt(level / math.sqrt(D))
    noise = jax.random.normal(jax.random.fold_in(key, salt + 3), (count, D), jnp.float32)
    strong = magnitude * common_direction(key)[None, :] + 0.3 * noise
    return jnp.where(chosen, strong, base)


def draw_source_points(key, part):
    noise = jax.random.normal(jax.random.fold_in(key, 1), (NS, D), jnp.float32)
    base = noise
    values = strong_rows(key, base, NS, 21)
    return jnp.clip(values, -8.0, 8.0).astype(jnp.bfloat16)


def draw_target_points(key, part):
    noise = jax.random.normal(jax.random.fold_in(key, 3), (NT, D), jnp.float32)
    base = noise
    values = strong_rows(key, base, NT, 31)
    return jnp.clip(values, -8.0, 8.0).astype(jnp.bfloat16)


def draw_tile_index(key, part):
    groups = RT * N_COL
    keys = jax.random.split(jax.random.fold_in(key, 11), groups)
    perms = jax.vmap(lambda one: jax.random.permutation(one, CTL))(keys).astype(jnp.int32)
    rows = jnp.arange(groups) // N_COL
    cols = jnp.arange(groups) % N_COL
    shifts = jax.random.randint(jax.random.fold_in(key, 12), (N_COL,), 0, CTL)
    target = ((rows + shifts[cols]) % CTL).astype(jnp.int32)
    rest = jnp.where(perms[:, 1:] == target[:, None], perms[:, :1], perms[:, 1:])
    listed = jnp.concatenate([target[:, None], rest], axis=1)[:, :KL]
    return listed.reshape(RT, N_COL * KL).astype(jnp.int32)


def draw_tile_count(key, part):
    counts = jax.random.randint(jax.random.fold_in(key, 13), (RT, N_COL), 1, KL + 1)
    picks = jax.random.randint(jax.random.fold_in(key, 14), (N_COL,), 0, SR // TILE)
    forced = jnp.arange(RT)[:, None] % (SR // TILE) == picks[None, :]
    return jnp.where(forced, KL, counts).astype(jnp.int32)


def block_scale(rng, dims, shards, least, top_value):
    def one(axis_at, blocks):
        draws = jax.random.uniform(jax.random.fold_in(jax.random.fold_in(rng, 6), axis_at), (blocks,), jnp.float32, least / len(shards), top_value / len(shards))
        return jnp.repeat(jnp.exp(draws), dims[axis_at] // blocks).reshape((-1,) + (1,) * (len(dims) - axis_at - 1))

    gain = one(*shards[0])
    for cut in shards[1:]:
        gain = gain * one(*cut)
    return gain


def setup_inputs(seed: int = 0) -> dict:
    key_list = jax.random.split(jax.random.key(seed), 7)
    return {
        "source_points": draw_source_points(jax.random.fold_in(key_list[6], 71), 0),
        "target_points": draw_target_points(jax.random.fold_in(key_list[6], 71), 0),
        "source_mass": jnp.clip(jnp.exp(math.log(4.0) - 2.7725887 * jax.random.uniform(key_list[2], (NS,), jnp.float32) ** block_scale(key_list[2], (NS,), ((0, 16),), -0.2, 0.2)), 0.25, 4.0),
        "target_mass": jnp.clip(jnp.exp(math.log(4.0) - 2.7725887 * jax.random.uniform(key_list[3], (NT,), jnp.float32) ** block_scale(key_list[3], (NT,), ((0, 8),), -0.2, 0.2)), 0.25, 4.0),
        "tile_index": draw_tile_index(jax.random.fold_in(key_list[6], 71), 0),
        "tile_count": draw_tile_count(jax.random.fold_in(key_list[6], 71), 0),
    }


def reference(source_points, target_points, source_mass, target_mass, tile_index, tile_count):
    masked_score = -1e+30
    col_tiles = TC // TILE
    total_tiles = NT // TILE
    slots = N_COL * KL
    offsets = (jnp.arange(slots) // KL * col_tiles).astype(jnp.int32)
    global_index = (tile_index + offsets[None, :]).astype(jnp.int32)
    live = (jnp.arange(slots) % KL)[None, :] < jnp.repeat(tile_count, KL, axis=1)
    target_tiles = target_points.reshape(total_tiles, TILE, D)
    source_tiles = source_points.reshape(RT, TILE, D)
    log_source = jnp.log(source_mass).reshape(RT, TILE)
    log_target = jnp.log(target_mass).reshape(total_tiles, TILE)
    scale = 1.0 / math.sqrt(D)
    target_pot = jnp.zeros((total_tiles, TILE), jnp.float32)
    row_pots = None
    for iteration in range(ITERS):

        def visit(carry, inputs, target_pot=target_pot):
            col_top, col_sum = carry
            rows, chosen, alive, log_row = inputs
            cost = jnp.einsum('ad,sbd->sab', rows.astype(jnp.float32), target_tiles[chosen].astype(jnp.float32), precision=lax.Precision.HIGHEST) * scale
            scores = jnp.where(alive[:, None, None], cost + target_pot[chosen][:, None, :], masked_score)
            top = lax.optimization_barrier(jnp.max(scores, axis=(0, 2)))
            total = lax.optimization_barrier(jnp.sum(jnp.exp(scores - top[None, :, None]), axis=(0, 2)))
            row_pot = log_row - top - jnp.log(total)
            columns = jnp.where(alive[:, None, None], cost + row_pot[None, :, None], masked_score)
            slot_top = lax.optimization_barrier(jnp.max(columns, axis=1))
            old_top = col_top[chosen]
            new_top = jnp.maximum(old_top, slot_top)
            sums = lax.optimization_barrier(jnp.sum(jnp.exp(columns - new_top[:, None, :]), axis=1))
            sums = jnp.where(alive[:, None], sums, 0.0)
            new_sum = col_sum[chosen] * jnp.exp(old_top - new_top) + sums
            col_top = col_top.at[chosen].set(new_top)
            col_sum = col_sum.at[chosen].set(new_sum)
            return ((col_top, col_sum), row_pot)
        start = (jnp.full((total_tiles, TILE), masked_score, jnp.float32), jnp.zeros((total_tiles, TILE), jnp.float32))
        (col_top, col_sum), row_pots = lax.scan(visit, start, (source_tiles, global_index, live, log_source))
        target_pot = log_target - col_top - jnp.log(col_sum)
    return (row_pots.reshape(-1), target_pot.reshape(-1))
```

```python
import functools
import math

import jax
import jax.numpy as jnp
from jax import lax
from jax.experimental import pallas as pl
from jax.experimental.pallas import tpu as pltpu
from jax.sharding import PartitionSpec as P

TILE = 256
ITERS = 3
LOG2E = 1.4426950408889634
LN2 = 0.6931471805599453
NEG = -1e30
MESH = pl.DeviceIdType.MESH
HALF = 2048
QUART = 1024


def log2(v):
    return jnp.log(v) * LOG2E


def kernel(
    nx, ny, ncol, parts,
    ti, tv, tc, sp, tp, sm, tm, f_out, g_out,
    X, T0, T1, T2, T3, S, ST, GB, FB, MS, QS, FV, RC, RR, IV,
    lsem, gs, gr, cs, cr, rs, rr,
):
    T = (T0, T1, T2, T3)
    row = lax.axis_index("row")
    col = lax.axis_index("col")
    nrow = nx * ny
    x, y = row // ny, lax.rem(row, ny)

    def at(dx, dy):
        return (lax.rem(x + dx + nx, nx) * ny + lax.rem(y + dy + ny, ny), col)

    def row_peer(k):
        return (lax.rem(row + k, nrow), col)

    def col_peer(k):
        return (row, lax.rem(col + k, ncol))

    load_x = pltpu.make_async_copy(sp, X, lsem.at[0])
    load_x.start()

    barrier = pltpu.get_barrier_semaphore()
    for k in range(1, nrow):
        pl.semaphore_signal(barrier, inc=1, device_id=row_peer(k), device_id_type=MESH)
    for k in range(1, ncol):
        pl.semaphore_signal(barrier, inc=1, device_id=col_peer(k), device_id_type=MESH)
    pl.semaphore_wait(barrier, nrow + ncol - 2)

    sent = []

    def rows(dy):
        return pl.ds(pl.multiple_of(lax.rem(y + dy + ny, ny) * 64, 64), 64)

    def send(src, dst, to):
        k = len(sent)
        c = pltpu.make_async_remote_copy(
            src_ref=src, dst_ref=dst, send_sem=gs.at[k], recv_sem=gr.at[k],
            device_id=to, device_id_type=MESH,
        )
        c.start()
        sent.append(c)
        return c

    A, B = pl.ds(0, HALF), pl.ds(HALF, HALF)
    A0, A1 = pl.ds(0, QUART), pl.ds(QUART, QUART)
    B0, B1 = pl.ds(HALF, QUART), pl.ds(HALF + QUART, QUART)

    def own(part):
        return tp.at[:, part]

    def along_y(src, d, part, dy):
        up = send(src, T[d].at[rows(dy), part], at(0, 1))
        down = send(src, T[d].at[rows(dy), part], at(0, -1))
        return up, down

    def along_x(src, part, dy):
        up = send(src, T[3].at[rows(dy), part], at(1, 0))
        down = send(src, T[1].at[rows(dy), part], at(-1, 0))
        return up, down

    def forward_y(pair, d, low, high):
        pair[0].wait_recv()
        a = send(T[d].at[rows(-1), low], T[d].at[rows(-1), low], at(0, 1))
        pair[1].wait_recv()
        b = send(T[d].at[rows(1), high], T[d].at[rows(1), high], at(0, -1))
        return a, b

    def forward_x(pair, dy, low, high):
        pair[0].wait_recv()
        a = send(T[3].at[rows(dy), low], T[2].at[rows(dy), low], at(1, 0))
        pair[1].wait_recv()
        b = send(T[1].at[rows(dy), high], T[2].at[rows(dy), high], at(-1, 0))
        return a, b

    def done(*pairs):
        for pair in pairs:
            for c in pair:
                c.wait_recv()

    scale = LOG2E / math.sqrt(sp.shape[1])

    def scores(d):
        cols = pl.ds(pl.multiple_of(lax.rem(x + d, nx) * 256, 256), 256)

        def body(t, carry):
            left = X[pl.ds(pl.multiple_of(t * TILE, TILE), TILE), cols]
            for s in range(2):
                u = ti[s, t]
                right = T[d][:, pl.ds(u * TILE, TILE)]
                new = jnp.dot(left, right, preferred_element_type=jnp.float32)
                p = s * 16 + t
                if d == 0:
                    S[p] = new
                elif d == 2:
                    new = (S[p] + new) * scale
                    S[p] = new
                    ST[p] = new.T
                else:
                    S[p] = S[p] + new
            return carry

        lax.fori_loop(0, 16, body, 0)

    if parts[0]:
        a1 = along_x(own(A), A, 0)
        b1 = along_y(own(B), 0, B, 0)
        ay0 = along_y(own(A), 0, A, 0)
        bx0 = along_x(own(B), B, 0)
    keep = pltpu.make_async_copy(tp, T[0].at[rows(0), :], lsem.at[1])
    keep.start()

    GB[...] = jnp.zeros_like(GB)
    diagonal = lax.broadcasted_iota(jnp.int32, (16, 16), 0) == lax.broadcasted_iota(jnp.int32, (16, 16), 1)
    for s in range(2):
        name = jnp.where(tc[...] > s, tv[s:s + 1, :], -1).astype(jnp.float32)
        down = jnp.sum(jnp.where(diagonal, jnp.broadcast_to(name, (16, 16)), 0.0), axis=1, keepdims=True)
        IV[s * 16:(s + 1) * 16, :] = jnp.broadcast_to(down, (16, 128))

    if parts[0]:
        a2 = forward_x(a1, 0, A0, A1)
        ay3 = along_y(T[3].at[rows(0), A], 3, A, 0)
        ay1 = along_y(T[1].at[rows(0), A], 1, A, 0)
        b2 = forward_y(b1, 0, B0, B1)
        bx3 = along_x(T[0].at[rows(-1), B], B, -1)
        bx1 = along_x(T[0].at[rows(1), B], B, 1)
        fay0 = forward_y(ay0, 0, A0, A1)
        fbx0 = forward_x(bx0, 0, B0, B1)
        done(a2)
        ay2 = along_y(T[2].at[rows(0), A], 2, A, 0)
        done(b2)
        bx2 = along_x(T[0].at[rows(2), B], B, 2)
        done(fay0)
    keep.wait()
    load_x.wait()
    if parts[1]:
        scores(0)
    if parts[0]:
        fay3 = forward_y(ay3, 3, A0, A1)
        fay1 = forward_y(ay1, 1, A0, A1)
        fbx3 = forward_x(bx3, -1, B0, B1)
        fbx1 = forward_x(bx1, 1, B0, B1)
        fay2 = forward_y(ay2, 2, A0, A1)
        fbx2 = forward_x(bx2, 2, B0, B1)
        done(fay3, fay1)
    if parts[1]:
        scores(3)
        scores(1)
    if parts[0]:
        done(fbx0, fbx3, fbx1, fay2, fbx2)
    if parts[1]:
        scores(2)

    def each_tile(src, add):
        def body(t, carry):
            for s in range(2):
                p = s * 16 + t
                for h in range(2):
                    r = src[p, :, h * 128:(h + 1) * 128] + add(s, t)
                    top = jnp.max(r, axis=0, keepdims=True)
                    total = jnp.sum(jnp.exp2(r - top), axis=0, keepdims=True)
                    MS[h, pl.ds(p, 1), :] = top
                    QS[h, pl.ds(p, 1), :] = total
            return carry

        lax.fori_loop(0, 16, body, 0)

    def spread(dst):
        def body(t, carry):
            for h in range(2):
                v = jnp.broadcast_to(FV[h, pl.ds(t, 1), :], (128, 128))
                dst[t, h * 128:(h + 1) * 128, :] = v.T
            return carry

        lax.fori_loop(0, 16, body, 0)

    def merged(got):
        top = jnp.max(got, axis=0)
        return top + log2(jnp.sum(jnp.exp2(got - top[None]), axis=0))

    def exchange(buf, it, me, n, peer, ss, rsem):
        copies = []
        for k in range(1, n):
            c = pltpu.make_async_remote_copy(
                src_ref=buf.at[it, me], dst_ref=buf.at[it, me],
                send_sem=ss.at[it, k], recv_sem=rsem.at[it, k],
                device_id=peer(k), device_id_type=MESH,
            )
            c.start()
            copies.append(c)
        for c in copies:
            c.wait()

    def iteration(it, carry):
        if parts[2]:
            each_tile(ST, lambda s, t: GB[ti[s, t]])
        for h in range(2):
            one = jnp.where(IV[...] < 0.0, NEG, MS[h] + log2(QS[h]))
            a, b = one[:16], one[16:]
            top = jnp.maximum(a, b)
            RC[it, col, h] = top + log2(jnp.exp2(a - top) + jnp.exp2(b - top))
        if parts[3]:
            exchange(RC, it, col, ncol, col_peer, cs, cr)
        for h in range(2):
            log_mass = log2(sm[pl.ds(h, 16, stride=2), :])
            f = log_mass - merged(RC[it, :, h])
            FV[h] = f
            f_out[pl.ds(h, 16, stride=2), :] = f
        if parts[2]:
            spread(FB)
            each_tile(S, lambda s, t: FB[t])
        for h in range(2):
            one = MS[h] + log2(QS[h])
            for u in range(16):
                named = IV[...] == float(u)
                top = jnp.max(jnp.where(named, one, NEG), axis=0, keepdims=True)
                total = jnp.sum(jnp.where(named, jnp.exp2(one - top), 0.0), axis=0, keepdims=True)
                RR[it, row, h, pl.ds(u, 1), :] = top + log2(jnp.maximum(total, 1e-30))
        if parts[4]:
            exchange(RR, it, row, nrow, row_peer, rs, rr)
        for h in range(2):
            log_mass = log2(tm[pl.ds(h, 16, stride=2), :])
            g = log_mass - merged(RR[it, :, h])
            FV[h] = g
            g_out[pl.ds(h, 16, stride=2), :] = g
        if parts[2]:
            spread(GB)
        return carry

    lax.fori_loop(0, ITERS, iteration, 0)
    for c in sent:
        c.wait_send()


def build(mesh, parts):
    ncol = mesh.shape["col"]
    nrow = mesh.shape["row"]
    nx = ny = math.isqrt(nrow)

    def on_device(source_points, target_points, source_mass, target_mass, tile_index, tile_count):
        n, d = source_points.shape
        m = target_points.shape[0]
        vmem = pl.BlockSpec(memory_space=pltpu.VMEM)
        smem = pl.BlockSpec(memory_space=pltpu.SMEM)
        hbm = pl.BlockSpec(memory_space=pl.ANY)
        f32 = jnp.float32
        f, g = pl.pallas_call(
            functools.partial(kernel, nx, ny, ncol, parts),
            out_shape=(
                jax.ShapeDtypeStruct((n // 128, 128), f32),
                jax.ShapeDtypeStruct((m // 128, 128), f32),
            ),
            in_specs=[smem, vmem, vmem, hbm, hbm, vmem, vmem],
            out_specs=(vmem, vmem),
            scratch_shapes=[
                pltpu.VMEM((n, d), jnp.bfloat16),
                *[pltpu.VMEM((256, m), jnp.bfloat16) for _ in range(4)],
                pltpu.VMEM((32, TILE, TILE), f32),
                pltpu.VMEM((32, TILE, TILE), f32),
                pltpu.VMEM((16, TILE, 128), f32),
                pltpu.VMEM((16, TILE, 128), f32),
                pltpu.VMEM((2, 32, 128), f32),
                pltpu.VMEM((2, 32, 128), f32),
                pltpu.VMEM((2, 16, 128), f32),
                pltpu.VMEM((ITERS, ncol, 2, 16, 128), f32),
                pltpu.VMEM((ITERS, nrow, 2, 16, 128), f32),
                pltpu.VMEM((32, 128), f32),
                pltpu.SemaphoreType.DMA((2,)),
                pltpu.SemaphoreType.DMA((40,)),
                pltpu.SemaphoreType.DMA((40,)),
                pltpu.SemaphoreType.DMA((ITERS, ncol)),
                pltpu.SemaphoreType.DMA((ITERS, ncol)),
                pltpu.SemaphoreType.DMA((ITERS, nrow)),
                pltpu.SemaphoreType.DMA((ITERS, nrow)),
            ],
            compiler_params=pltpu.CompilerParams(
                collective_id=0, has_side_effects=True, vmem_limit_bytes=60 * 2**20
            ),
        )(
            tile_index.T, tile_index.T, tile_count.T, source_points, target_points.T,
            source_mass.reshape(-1, 128), target_mass.reshape(-1, 128),
        )
        return (f * LN2).reshape(-1), (g * LN2).reshape(-1)

    placed = (P("row", None), P("col", "row"), P("row"), P("col"), P("row", "col"), P("row", "col"))
    return jax.shard_map(
        on_device, mesh=mesh, in_specs=placed, out_specs=(P("row"), P("col")), check_vma=False
    )


def solution(mesh):
    return build(mesh, (True,) * 5)
```

```python
import functools
import math

import jax
import jax.numpy as jnp
from jax import lax
from jax.experimental import pallas as pl
from jax.experimental.pallas import tpu as pltpu
from jax.sharding import PartitionSpec as P

TILE = 256
ITERS = 3
LOG2E = 1.4426950408889634
LN2 = 0.6931471805599453
NEG = -1e30
MESH = pl.DeviceIdType.MESH
HALF = 2048
QUART = 1024


def log2(v):
    return jnp.log(v) * LOG2E


def kernel(
    nx, ny, ncol, parts,
    ti, tc, tv, cv, sp, tp, sm, tm, f_out, g_out,
    X, T0, T1, T2, T3, S, MB, FB, MS, QS, M8, W8, FV, GV, UV, RC, RR, IV,
    lsem, gs, gr, cr, rs, es,
):
    T = (T0, T1, T2, T3)
    row = lax.axis_index("row")
    col = lax.axis_index("col")
    nrow = nx * ny
    x, y = row // ny, lax.rem(row, ny)

    def at(dx, dy):
        return (lax.rem(x + dx + nx, nx) * ny + lax.rem(y + dy + ny, ny), col)

    def row_peer(k):
        return (lax.rem(row + k, nrow), col)

    def col_peer(k):
        return (row, lax.rem(col + k, ncol))

    load_x = pltpu.make_async_copy(sp, X, lsem.at[0])
    load_x.start()

    barrier = pltpu.get_barrier_semaphore()
    for k in range(1, nrow):
        pl.semaphore_signal(barrier, inc=1, device_id=row_peer(k), device_id_type=MESH)
    for k in range(1, ncol):
        pl.semaphore_signal(barrier, inc=1, device_id=col_peer(k), device_id_type=MESH)
    pl.semaphore_wait(barrier, nrow + ncol - 2)

    used = []

    def rows(dy):
        return pl.ds(pl.multiple_of(lax.rem(y + dy + ny, ny) * 64, 64), 64)

    steps = {0: (1, 0), 1: (-1, 0), 2: (0, 1), 3: (0, -1)}

    def fresh():
        used.append(0)
        return len(used) - 1

    def send(src, dst, link, k=None):
        k = fresh() if k is None else k
        c = pltpu.make_async_remote_copy(
            src_ref=src, dst_ref=dst, send_sem=gs.at[link], recv_sem=gr.at[k],
            device_id=at(*steps[link]), device_id_type=MESH,
        )
        c.start()
        return c

    A, B = pl.ds(0, HALF), pl.ds(HALF, HALF)
    A0, A1 = pl.ds(0, QUART), pl.ds(QUART, QUART)
    B0, B1 = pl.ds(HALF, QUART), pl.ds(HALF + QUART, QUART)

    def own(part):
        return tp.at[:, part]

    def along_y(src, d, part, dy):
        return tuple(send(src, T[d].at[rows(dy), part], link) for link in (2, 3))

    def along_x(src, part, dy):
        return (
            send(src, T[3].at[rows(dy), part], 0),
            send(src, T[1].at[rows(dy), part], 1),
        )

    def forward_y(pair, d, low, high):
        k = fresh()
        pair[0].wait_recv()
        send(T[d].at[rows(-1), low], T[d].at[rows(-1), low], 2, k)
        pair[1].wait_recv()
        send(T[d].at[rows(1), high], T[d].at[rows(1), high], 3, k)
        return k

    def forward_x(pair, dy, low, high):
        k = fresh()
        pair[0].wait_recv()
        send(T[3].at[rows(dy), low], T[2].at[rows(dy), low], 0, k)
        pair[1].wait_recv()
        send(T[1].at[rows(dy), high], T[2].at[rows(dy), high], 1, k)
        return k

    def done(*sems):
        for k in sems:
            whole = T[0].at[rows(0), A]
            pltpu.make_async_copy(whole, whole, gr.at[k]).wait()

    scale = LOG2E / math.sqrt(sp.shape[1])
    wide = (32, 8, 128)
    diagonal = lax.broadcasted_iota(jnp.int32, (128, 128), 0) == lax.broadcasted_iota(jnp.int32, (128, 128), 1)

    def to_row(v):
        return jnp.sum(jnp.where(diagonal, jnp.broadcast_to(v, (128, 128)), 0.0), axis=0, keepdims=True)

    def product(d, t, s):
        cols = pl.ds(pl.multiple_of(lax.rem(x + d, nx) * 256, 256), 256)
        left = X[pl.ds(pl.multiple_of(t * TILE, TILE), TILE), cols]
        right = T[d][:, pl.ds(ti[s, t] * TILE, TILE)]
        return jnp.dot(left, right, preferred_element_type=jnp.float32) * scale

    def scores(d):
        def body(t, carry):
            for s in range(2):
                p = s * 16 + t
                new = product(d, t, s)
                S[p] = new if d == 0 else S[p] + new
            return carry

        lax.fori_loop(0, 16, body, 0)

    def idle(t):
        return (tc[0, t].astype(jnp.float32) - 2.0) * 1e30

    if parts[0]:
        a1 = along_x(own(A), A, 0)
        b1 = along_y(own(B), 0, B, 0)
        ay0 = along_y(own(A), 0, A, 0)
        bx0 = along_x(own(B), B, 0)
    keep = pltpu.make_async_copy(tp, T[0].at[rows(0), :], lsem.at[1])
    keep.start()

    small = lax.broadcasted_iota(jnp.int32, (16, 16), 0) == lax.broadcasted_iota(jnp.int32, (16, 16), 1)
    for s in range(2):
        name = jnp.where(cv[...] > s, tv[s:s + 1, :], -1).astype(jnp.float32)
        down = jnp.sum(jnp.where(small, jnp.broadcast_to(name, (16, 16)), 0.0), axis=1, keepdims=True)
        IV[s * 16:(s + 1) * 16, :] = jnp.broadcast_to(down, (16, 128))

    if parts[0]:
        a2 = forward_x(a1, 0, A0, A1)
        ay3 = along_y(T[3].at[rows(0), A], 3, A, 0)
        ay1 = along_y(T[1].at[rows(0), A], 1, A, 0)
        b2 = forward_y(b1, 0, B0, B1)
        bx3 = along_x(T[0].at[rows(-1), B], B, -1)
        bx1 = along_x(T[0].at[rows(1), B], B, 1)
        fay0 = forward_y(ay0, 0, A0, A1)
        fbx0 = forward_x(bx0, 0, B0, B1)
        done(a2)
        ay2 = along_y(T[2].at[rows(0), A], 2, A, 0)
        done(b2)
        bx2 = along_x(T[0].at[rows(2), B], B, 2)
        done(fay0)
    keep.wait()
    load_x.wait()
    if parts[1]:
        scores(0)
    if parts[0]:
        fay3 = forward_y(ay3, 3, A0, A1)
        fay1 = forward_y(ay1, 1, A0, A1)
        fbx3 = forward_x(bx3, -1, B0, B1)
        fbx1 = forward_x(bx1, 1, B0, B1)
        fay2 = forward_y(ay2, 2, A0, A1)
        fbx2 = forward_x(bx2, 2, B0, B1)
        done(fay3, fay1)
    if parts[1]:
        scores(3)
        scores(1)
    if parts[0]:
        done(fbx0, fbx3, fbx1, fay2, fbx2)

    def finish(t):
        tops = []
        for s in range(2):
            p = s * 16 + t
            r = S[p] + product(2, t, s)
            S[p] = r
            tops.append(jnp.maximum(r[:, :128], r[:, 128:]))
        top = jnp.max(jnp.maximum(tops[0], tops[1] + idle(t)), axis=1, keepdims=True)
        MB[lax.rem(t, 2)] = jnp.broadcast_to(top, (TILE, 128))

    def row_logs(t):
        top = MB[lax.rem(t, 2)]
        total = jnp.zeros((TILE, 128), jnp.float32)
        for s in range(2):
            shift = top if s == 0 else top - idle(t)
            for h in range(2):
                total += jnp.exp2(S[s * 16 + t, :, h * 128:(h + 1) * 128] - shift)
        value = top[:, :1] + log2(jnp.sum(total, axis=1, keepdims=True))
        for h in range(2):
            RC[0, col, h, pl.ds(t, 1), :] = to_row(value[h * 128:(h + 1) * 128])

    if parts[1]:
        finish(0)

        def step(t, carry):
            finish(t)
            row_logs(t - 1)
            return carry

        lax.fori_loop(1, 16, step, 0)
        row_logs(15)

    def spread(t):
        for h in range(2):
            v = jnp.broadcast_to(UV[h, pl.ds(t, 1), :], (128, 128))
            FB[t, h * 128:(h + 1) * 128, :] = v.T

    def each_tile(visit):
        spread(0)

        def body(t, carry):
            spread(lax.min(t + 1, 15))
            visit(t)
            return carry

        lax.fori_loop(0, 16, body, 0)

    def block(p, h):
        return S[p, :, h * 128:(h + 1) * 128].reshape(wide)

    def column_logs(t):
        add = FB[t].reshape(wide)
        for s in range(2):
            p = s * 16 + t
            for h in range(2):
                c = block(p, h) + add
                m8 = jnp.max(c, axis=0)
                e = jnp.exp2(c - m8[None])
                S[p, :, h * 128:(h + 1) * 128] = e.reshape(TILE, 128)
                M8[h, p] = m8
                s8 = jnp.sum(e, axis=0)
                top = jnp.max(m8, axis=0, keepdims=True)
                MS[h, pl.ds(p, 1), :] = top
                QS[h, pl.ds(p, 1), :] = jnp.sum(s8 * jnp.exp2(m8 - top), axis=0, keepdims=True)

    def row_sums(it):
        def body(t, carry):
            total = jnp.zeros(wide, jnp.float32)
            for s in range(2):
                p = s * 16 + t
                for h in range(2):
                    total += block(p, h) * W8[h, p][None]
            value = jnp.sum(total.reshape(TILE, 128), axis=1, keepdims=True)
            for h in range(2):
                RC[it, col, h, pl.ds(t, 1), :] = to_row(value[h * 128:(h + 1) * 128])
            return carry

        lax.fori_loop(0, 16, body, 0, unroll=2)

    def column_sums(t):
        by = FB[t].reshape(wide)
        for s in range(2):
            p = s * 16 + t
            for h in range(2):
                s8 = jnp.sum(block(p, h) * by, axis=0) * W8[h, p]
                QS[h, pl.ds(p, 1), :] = jnp.sum(s8, axis=0, keepdims=True)

    def merged(got):
        top = jnp.max(got, axis=0)
        return top + log2(jnp.sum(jnp.exp2(got - top[None]), axis=0))

    def exchange(buf, it, me, n, peer, rsem):
        for k in range(1, n):
            pltpu.make_async_remote_copy(
                src_ref=buf.at[it, me], dst_ref=buf.at[it, me],
                send_sem=es.at[0], recv_sem=rsem.at[it],
                device_id=peer(k), device_id_type=MESH,
            ).start()
        others = buf.at[it, pl.ds(0, n - 1)]
        pltpu.make_async_copy(others, others, rsem.at[it]).wait()

    def mass(ref, h):
        return ref[pl.ds(h, 16, stride=2), :]

    def put(ref, h, v):
        ref[pl.ds(h, 16, stride=2), :] = v

    if parts[3]:
        exchange(RC, 0, col, ncol, col_peer, cr)
    for h in range(2):
        f = log2(mass(sm, h)) - merged(RC[0, :, h])
        FV[h] = f
        UV[h] = f
    if parts[2]:
        each_tile(column_logs)
    for h in range(2):
        one = MS[h] + log2(QS[h])
        for u in range(16):
            named = IV[...] == float(u)
            top = jnp.max(jnp.where(named, one, NEG), axis=0, keepdims=True)
            total = jnp.sum(jnp.where(named, jnp.exp2(one - top), 0.0), axis=0, keepdims=True)
            RR[0, row, h, pl.ds(u, 1), :] = top + log2(jnp.maximum(total, 1e-30))
    if parts[4]:
        exchange(RR, 0, row, nrow, row_peer, rs)
    for h in range(2):
        GV[h] = log2(mass(tm, h)) - merged(RR[0, :, h])

    def weigh(first):
        def body(t, carry):
            for s in range(2):
                p = s * 16 + t
                for h in range(2):
                    if first:
                        g = GV[h, pl.ds(ti[s, t], 1), :]
                        W8[h, p] = jnp.exp2(M8[h, p] + (g if s == 0 else g + idle(t)))
                    else:
                        W8[h, p] = W8[h, p] * UV[h, pl.ds(ti[s, t], 1), :]
            return carry

        lax.fori_loop(0, 16, body, 0, unroll=4)

    for it in range(1, ITERS):
        if parts[2]:
            weigh(it == 1)
            row_sums(it)
        if parts[3]:
            exchange(RC, it, col, ncol, col_peer, cr)
        for h in range(2):
            u = mass(sm, h) / jnp.sum(RC[it, :, h], axis=0)
            UV[h] = u
            if it == ITERS - 1:
                put(f_out, h, (FV[h] + log2(u)) * LN2)
        if parts[2]:
            each_tile(column_sums)
        for h in range(2):
            one = QS[h]
            for u in range(16):
                named = IV[...] == float(u)
                RR[it, row, h, pl.ds(u, 1), :] = jnp.sum(jnp.where(named, one, 0.0), axis=0, keepdims=True)
        if parts[4]:
            exchange(RR, it, row, nrow, row_peer, rs)
        for h in range(2):
            v = mass(tm, h) / jnp.sum(RR[it, :, h], axis=0)
            UV[h] = v
            GV[h] = GV[h] + log2(v)
            if it == ITERS - 1:
                put(g_out, h, GV[h] * LN2)

    if parts[0]:
        for link in range(4):
            quarter = X.at[pl.ds(0, 960)]
            pltpu.make_async_copy(quarter, quarter, gs.at[link]).wait()
    if parts[3] and parts[4]:
        sent = X.at[pl.ds(0, 8 * ITERS * (nrow + ncol - 2))]
        pltpu.make_async_copy(sent, sent, es.at[0]).wait()


def build(mesh, parts):
    ncol = mesh.shape["col"]
    nrow = mesh.shape["row"]
    nx = ny = math.isqrt(nrow)

    def on_device(source_points, target_points, source_mass, target_mass, tile_index, tile_count):
        n, d = source_points.shape
        m = target_points.shape[0]
        vmem = pl.BlockSpec(memory_space=pltpu.VMEM)
        smem = pl.BlockSpec(memory_space=pltpu.SMEM)
        hbm = pl.BlockSpec(memory_space=pl.ANY)
        f32 = jnp.float32
        f, g = pl.pallas_call(
            functools.partial(kernel, nx, ny, ncol, parts),
            out_shape=(
                jax.ShapeDtypeStruct((n // 128, 128), f32),
                jax.ShapeDtypeStruct((m // 128, 128), f32),
            ),
            in_specs=[smem, smem, vmem, vmem, hbm, hbm, vmem, vmem],
            out_specs=(vmem, vmem),
            scratch_shapes=[
                pltpu.VMEM((n, d), jnp.bfloat16),
                *[pltpu.VMEM((256, m), jnp.bfloat16) for _ in range(4)],
                pltpu.VMEM((32, TILE, TILE), f32),
                pltpu.VMEM((2, TILE, 128), f32),
                pltpu.VMEM((16, TILE, 128), f32),
                pltpu.VMEM((2, 32, 128), f32),
                pltpu.VMEM((2, 32, 128), f32),
                pltpu.VMEM((2, 32, 8, 128), f32),
                pltpu.VMEM((2, 32, 8, 128), f32),
                pltpu.VMEM((2, 16, 128), f32),
                pltpu.VMEM((2, 16, 128), f32),
                pltpu.VMEM((2, 16, 128), f32),
                pltpu.VMEM((ITERS, ncol, 2, 16, 128), f32),
                pltpu.VMEM((ITERS, nrow, 2, 16, 128), f32),
                pltpu.VMEM((32, 128), f32),
                pltpu.SemaphoreType.DMA((2,)),
                pltpu.SemaphoreType.DMA((4,)),
                pltpu.SemaphoreType.DMA((30,)),
                pltpu.SemaphoreType.DMA((ITERS,)),
                pltpu.SemaphoreType.DMA((ITERS,)),
                pltpu.SemaphoreType.DMA((1,)),
            ],
            compiler_params=pltpu.CompilerParams(
                collective_id=0, has_side_effects=True, vmem_limit_bytes=60 * 2**20
            ),
        )(
            tile_index.T, tile_count.T, tile_index.T, tile_count.T, source_points, target_points.T,
            source_mass.reshape(-1, 128), target_mass.reshape(-1, 128),
        )
        return f.reshape(-1), g.reshape(-1)

    placed = (P("row", None), P("col", "row"), P("row"), P("col"), P("row", "col"), P("row", "col"))
    return jax.shard_map(
        on_device, mesh=mesh, in_specs=placed, out_specs=(P("row"), P("col")), check_vma=False
    )


def solution(mesh):
    return build(mesh, (True,) * 5)
```

```python
import functools
import math

import jax
import jax.numpy as jnp
from jax import lax
from jax.experimental import pallas as pl
from jax.experimental.pallas import tpu as pltpu
from jax.sharding import PartitionSpec as P

TILE = 256
ITERS = 3
LOG2E = 1.4426950408889634
LN2 = 0.6931471805599453
NEG = -1e30
MESH = pl.DeviceIdType.MESH
HALF = 2048
QUART = 1024


def log2(v):
    return jnp.log(v) * LOG2E


def kernel(
    nx, ny, ncol, parts,
    ti, tc, tv, cv, sp, tp, sm, tm, f_out, g_out,
    X, T0, T1, T2, T3, S, SP, KA, KB, TB, MA, MC, MS, QS, M8, W8, FV, GV, UV, RC, RR, IV,
    lsem, gs, gr, cr, rs, es,
):
    T = (T0, T1, T2, T3)
    row = lax.axis_index("row")
    col = lax.axis_index("col")
    nrow = nx * ny
    x, y = row // ny, lax.rem(row, ny)

    def at(dx, dy):
        return (lax.rem(x + dx + nx, nx) * ny + lax.rem(y + dy + ny, ny), col)

    def row_peer(k):
        return (lax.rem(row + k, nrow), col)

    def col_peer(k):
        return (row, lax.rem(col + k, ncol))

    load_x = pltpu.make_async_copy(sp, X, lsem.at[0])
    load_x.start()

    barrier = pltpu.get_barrier_semaphore()
    for k in range(1, nrow):
        pl.semaphore_signal(barrier, inc=1, device_id=row_peer(k), device_id_type=MESH)
    for k in range(1, ncol):
        pl.semaphore_signal(barrier, inc=1, device_id=col_peer(k), device_id_type=MESH)
    pl.semaphore_wait(barrier, nrow + ncol - 2)

    used = []

    def rows(dy):
        return pl.ds(pl.multiple_of(lax.rem(y + dy + ny, ny) * 64, 64), 64)

    steps = {0: (1, 0), 1: (-1, 0), 2: (0, 1), 3: (0, -1)}

    def fresh():
        used.append(0)
        return len(used) - 1

    def send(src, dst, link, k=None):
        k = fresh() if k is None else k
        c = pltpu.make_async_remote_copy(
            src_ref=src, dst_ref=dst, send_sem=gs.at[link], recv_sem=gr.at[k],
            device_id=at(*steps[link]), device_id_type=MESH,
        )
        c.start()
        return c

    A, B = pl.ds(0, HALF), pl.ds(HALF, HALF)
    A0, A1 = pl.ds(0, QUART), pl.ds(QUART, QUART)
    B0, B1 = pl.ds(HALF, QUART), pl.ds(HALF + QUART, QUART)

    def own(part):
        return tp.at[:, part]

    def along_y(src, d, part, dy):
        return tuple(send(src, T[d].at[rows(dy), part], link) for link in (2, 3))

    def along_x(src, part, dy):
        return (
            send(src, T[3].at[rows(dy), part], 0),
            send(src, T[1].at[rows(dy), part], 1),
        )

    def forward_y(pair, d, low, high):
        k = fresh()
        pair[0].wait_recv()
        send(T[d].at[rows(-1), low], T[d].at[rows(-1), low], 2, k)
        pair[1].wait_recv()
        send(T[d].at[rows(1), high], T[d].at[rows(1), high], 3, k)
        return k

    def forward_x(pair, dy, low, high):
        k = fresh()
        pair[0].wait_recv()
        send(T[3].at[rows(dy), low], T[2].at[rows(dy), low], 0, k)
        pair[1].wait_recv()
        send(T[1].at[rows(dy), high], T[2].at[rows(dy), high], 1, k)
        return k

    def done(*sems):
        for k in sems:
            whole = T[0].at[rows(0), A]
            pltpu.make_async_copy(whole, whole, gr.at[k]).wait()

    scale = LOG2E / math.sqrt(sp.shape[1])
    wide = (32, 8, 128)

    def fold(op, v):
        v = v.reshape((v.shape[0] // 4, 4) + v.shape[1:])
        v = functools.reduce(op, [v[k] for k in range(v.shape[0])])
        while v.shape[0] > 1:
            n = v.shape[0] // 2
            v = op(v[:n], v[n:])
        return v[0]

    def product(chunks, t, s):
        here = pl.ds(pl.multiple_of(t * TILE, TILE), TILE)
        left = [X[here, pl.ds(pl.multiple_of(lax.rem(x + d, nx) * 256, 256), 256)] for d in chunks]
        right = [T[d][:, pl.ds(ti[s, t] * TILE, TILE)] for d in chunks]
        return jnp.dot(
            jnp.concatenate(left, axis=1), jnp.concatenate(right, axis=0), preferred_element_type=jnp.float32
        ) * scale

    def scores(*chunks):
        def body(t, carry):
            for s in range(2):
                p = s * 16 + t
                new = product(chunks, t, s)
                SP[p] = new if chunks == (0,) else SP[p] + new
            return carry

        lax.fori_loop(0, 16, body, 0)

    def idle(t):
        return (tc[0, t].astype(jnp.float32) - 2.0) * 1e30

    if parts[0]:
        a1 = along_x(own(A), A, 0)
        b1 = along_y(own(B), 0, B, 0)
        ay0 = along_y(own(A), 0, A, 0)
        bx0 = along_x(own(B), B, 0)
    keep = pltpu.make_async_copy(tp, T[0].at[rows(0), :], lsem.at[1])
    keep.start()

    small = lax.broadcasted_iota(jnp.int32, (16, 16), 0) == lax.broadcasted_iota(jnp.int32, (16, 16), 1)
    for s in range(2):
        name = jnp.where(cv[...] > s, tv[s:s + 1, :], -1).astype(jnp.float32)
        down = jnp.sum(jnp.where(small, jnp.broadcast_to(name, (16, 16)), 0.0), axis=1, keepdims=True)
        IV[s * 16:(s + 1) * 16, :] = jnp.broadcast_to(down, (16, 128))

    if parts[0]:
        a2 = forward_x(a1, 0, A0, A1)
        ay3 = along_y(T[3].at[rows(0), A], 3, A, 0)
        ay1 = along_y(T[1].at[rows(0), A], 1, A, 0)
        b2 = forward_y(b1, 0, B0, B1)
        bx3 = along_x(T[0].at[rows(-1), B], B, -1)
        bx1 = along_x(T[0].at[rows(1), B], B, 1)
        fay0 = forward_y(ay0, 0, A0, A1)
        fbx0 = forward_x(bx0, 0, B0, B1)
        done(a2)
        ay2 = along_y(T[2].at[rows(0), A], 2, A, 0)
        done(b2)
        bx2 = along_x(T[0].at[rows(2), B], B, 2)
        done(fay0)
    keep.wait()
    load_x.wait()
    if parts[1]:
        scores(0)
    if parts[0]:
        fay3 = forward_y(ay3, 3, A0, A1)
        fay1 = forward_y(ay1, 1, A0, A1)
        fbx3 = forward_x(bx3, -1, B0, B1)
        fbx1 = forward_x(bx1, 1, B0, B1)
        fay2 = forward_y(ay2, 2, A0, A1)
        fbx2 = forward_x(bx2, 2, B0, B1)
        done(fay3, fay1)
    if parts[1]:
        scores(3, 1)
    if parts[0]:
        done(fbx0, fbx3, fbx1, fay2, fbx2)

    def over_lanes(op, v):
        v = fold(op, v.T.reshape(16, 8, 128))
        n = 8
        while n > 1:
            n //= 2
            v = op(v[:n], v[n:])
        return v

    def as_column(v):
        return jnp.broadcast_to(v, (128, 128)).T

    def finish(t, K):
        tops = []
        for s in range(2):
            p = s * 16 + t
            r = SP[p] + product((2,), t, s)
            if s:
                r = r + idle(t)
            for h in range(2):
                S[h, p] = r[:, h * 128:(h + 1) * 128]
                K[s, h] = r[:, h * 128:(h + 1) * 128]
            tops.append(jnp.maximum(r[:, :128], r[:, 128:]))
        TB[...] = jnp.maximum(tops[0], tops[1])

    def row_tops(t):
        for h in range(2):
            part = slice(h * 128, (h + 1) * 128)
            line = over_lanes(jnp.maximum, TB[part, :])
            MS[h, pl.ds(t, 1), :] = line
            MA[part, :] = as_column(line)

    def row_exps(K):
        top = MA[...]
        e = [jnp.exp2(K[s, k] - top) for s in range(2) for k in range(2)]
        MC[...] = (e[0] + e[1]) + (e[2] + e[3])

    def row_totals(t):
        for h in range(2):
            QS[h, pl.ds(t, 1), :] = over_lanes(jnp.add, MC[h * 128:(h + 1) * 128, :])

    if parts[1]:
        def stages(t, K, now):
            if 3 in now:
                row_totals(t - 3)
            if 2 in now:
                row_exps(K)
            if 1 in now:
                row_tops(t - 1)
            if 0 in now:
                finish(t, K)

        def step(k, carry):
            stages(2 * k, KA, (3, 2, 1, 0))
            stages(2 * k + 1, KB, (3, 2, 1, 0))
            return carry

        stages(0, KA, (0,))
        stages(1, KB, (1, 0))
        stages(2, KA, (2, 1, 0))
        stages(3, KB, (3, 2, 1, 0))
        lax.fori_loop(2, 8, step, 0)
        stages(16, KA, (3, 2, 1))
        stages(17, KB, (3, 2))
        stages(18, KA, (3,))
    for h in range(2):
        RC[0, col, h] = MS[h, :16] + log2(QS[h, :16])

    def spread(t, to):
        for h in range(2):
            to[h * 128:(h + 1) * 128, :] = as_column(UV[h, pl.ds(t, 1), :])

    def each_tile(visit):
        spread(0, MA)

        def body(k, carry):
            t = 2 * k
            spread(t + 1, MC)
            visit(t, MA)
            spread(lax.min(t + 2, 15), MA)
            visit(t + 1, MC)
            return carry

        lax.fori_loop(0, 8, body, 0)

    def block(p, h):
        return S[h, p].reshape(wide)

    def column_logs(t, by):
        add = by[...].reshape(wide)
        for s in range(2):
            p = s * 16 + t
            for h in range(2):
                c = block(p, h) + add
                m8 = fold(jnp.maximum, c)
                e = jnp.exp2(c - m8[None])
                S[h, p] = e.reshape(TILE, 128)
                M8[h, p] = m8
                s8 = fold(jnp.add, e)
                top = jnp.max(m8, axis=0, keepdims=True)
                MS[h, pl.ds(p, 1), :] = top
                QS[h, pl.ds(p, 1), :] = jnp.sum(s8 * jnp.exp2(m8 - top), axis=0, keepdims=True)

    def row_sums(it):
        def body(t, carry):
            e = [block(s * 16 + t, h) * W8[h, s * 16 + t][None] for s in range(2) for h in range(2)]
            total = (e[0] + e[1]) + (e[2] + e[3])
            total = total.reshape(TILE, 128)
            for h in range(2):
                RC[it, col, h, pl.ds(t, 1), :] = over_lanes(jnp.add, total[h * 128:(h + 1) * 128])
            return carry

        lax.fori_loop(0, 16, body, 0, unroll=2)

    def column_sums(t, by):
        by = by[...].reshape(wide)
        for s in range(2):
            p = s * 16 + t
            for h in range(2):
                s8 = fold(jnp.add, block(p, h) * by) * W8[h, p]
                QS[h, pl.ds(p, 1), :] = jnp.sum(s8, axis=0, keepdims=True)

    def merged(got):
        top = jnp.max(got, axis=0)
        return top + log2(jnp.sum(jnp.exp2(got - top[None]), axis=0))

    def exchange(buf, it, me, n, peer, rsem):
        for k in range(1, n):
            pltpu.make_async_remote_copy(
                src_ref=buf.at[it, me], dst_ref=buf.at[it, me],
                send_sem=es.at[0], recv_sem=rsem.at[it],
                device_id=peer(k), device_id_type=MESH,
            ).start()
        others = buf.at[it, pl.ds(0, n - 1)]
        pltpu.make_async_copy(others, others, rsem.at[it]).wait()

    def mass(ref, h):
        return ref[pl.ds(h, 16, stride=2), :]

    def put(ref, h, v):
        ref[pl.ds(h, 16, stride=2), :] = v

    if parts[3]:
        exchange(RC, 0, col, ncol, col_peer, cr)
    for h in range(2):
        f = log2(mass(sm, h)) - merged(RC[0, :, h])
        FV[h] = f
        UV[h] = f
    if parts[2]:
        each_tile(column_logs)
    for h in range(2):
        one = MS[h] + log2(QS[h])
        for u in range(16):
            named = IV[...] == float(u)
            top = jnp.max(jnp.where(named, one, NEG), axis=0, keepdims=True)
            total = jnp.sum(jnp.where(named, jnp.exp2(one - top), 0.0), axis=0, keepdims=True)
            RR[0, row, h, pl.ds(u, 1), :] = top + log2(jnp.maximum(total, 1e-30))
    if parts[4]:
        exchange(RR, 0, row, nrow, row_peer, rs)
    for h in range(2):
        GV[h] = log2(mass(tm, h)) - merged(RR[0, :, h])

    def weigh(first):
        def body(t, carry):
            for s in range(2):
                p = s * 16 + t
                for h in range(2):
                    if first:
                        g = GV[h, pl.ds(ti[s, t], 1), :]
                        W8[h, p] = jnp.exp2(M8[h, p] + (g if s == 0 else g + idle(t)))
                    else:
                        W8[h, p] = W8[h, p] * UV[h, pl.ds(ti[s, t], 1), :]
            return carry

        lax.fori_loop(0, 16, body, 0, unroll=4)

    for it in range(1, ITERS):
        if parts[2]:
            weigh(it == 1)
            row_sums(it)
        if parts[3]:
            exchange(RC, it, col, ncol, col_peer, cr)
        for h in range(2):
            u = mass(sm, h) / jnp.sum(RC[it, :, h], axis=0)
            UV[h] = u
            if it == ITERS - 1:
                put(f_out, h, FV[h] + log2(u))
        if parts[2]:
            each_tile(column_sums)
        for h in range(2):
            one = QS[h]
            for u in range(16):
                named = IV[...] == float(u)
                RR[it, row, h, pl.ds(u, 1), :] = jnp.sum(jnp.where(named, one, 0.0), axis=0, keepdims=True)
        if parts[4]:
            exchange(RR, it, row, nrow, row_peer, rs)
        for h in range(2):
            v = mass(tm, h) / jnp.sum(RR[it, :, h], axis=0)
            UV[h] = v
            GV[h] = GV[h] + log2(v)
            if it == ITERS - 1:
                put(g_out, h, GV[h])

    if parts[0]:
        for link in range(4):
            quarter = X.at[pl.ds(0, 960)]
            pltpu.make_async_copy(quarter, quarter, gs.at[link]).wait()
    if parts[3] and parts[4]:
        sent = X.at[pl.ds(0, 8 * ITERS * (nrow + ncol - 2))]
        pltpu.make_async_copy(sent, sent, es.at[0]).wait()


def build(mesh, parts):
    ncol = mesh.shape["col"]
    nrow = mesh.shape["row"]
    nx = ny = math.isqrt(nrow)

    def on_device(source_points, target_points, source_mass, target_mass, tile_index, tile_count):
        n, d = source_points.shape
        m = target_points.shape[0]
        vmem = pl.BlockSpec(memory_space=pltpu.VMEM)
        smem = pl.BlockSpec(memory_space=pltpu.SMEM)
        hbm = pl.BlockSpec(memory_space=pl.ANY)
        f32 = jnp.float32
        f, g = pl.pallas_call(
            functools.partial(kernel, nx, ny, ncol, parts),
            out_shape=(
                jax.ShapeDtypeStruct((n // 128, 128), f32),
                jax.ShapeDtypeStruct((m // 128, 128), f32),
            ),
            in_specs=[smem, smem, vmem, vmem, hbm, hbm, vmem, vmem],
            out_specs=(vmem, vmem),
            scratch_shapes=[
                pltpu.VMEM((n, d), jnp.bfloat16),
                *[pltpu.VMEM((256, m), jnp.bfloat16) for _ in range(4)],
                pltpu.VMEM((2, 32, TILE, 128), f32),
                pltpu.VMEM((32, TILE, TILE), f32),
                pltpu.VMEM((2, 2, TILE, 128), f32),
                pltpu.VMEM((2, 2, TILE, 128), f32),
                pltpu.VMEM((TILE, 128), f32),
                pltpu.VMEM((TILE, 128), f32),
                pltpu.VMEM((TILE, 128), f32),
                pltpu.VMEM((2, 32, 128), f32),
                pltpu.VMEM((2, 32, 128), f32),
                pltpu.VMEM((2, 32, 8, 128), f32),
                pltpu.VMEM((2, 32, 8, 128), f32),
                pltpu.VMEM((2, 16, 128), f32),
                pltpu.VMEM((2, 16, 128), f32),
                pltpu.VMEM((2, 16, 128), f32),
                pltpu.VMEM((ITERS, ncol, 2, 16, 128), f32),
                pltpu.VMEM((ITERS, nrow, 2, 16, 128), f32),
                pltpu.VMEM((32, 128), f32),
                pltpu.SemaphoreType.DMA((2,)),
                pltpu.SemaphoreType.DMA((4,)),
                pltpu.SemaphoreType.DMA((30,)),
                pltpu.SemaphoreType.DMA((ITERS,)),
                pltpu.SemaphoreType.DMA((ITERS,)),
                pltpu.SemaphoreType.DMA((1,)),
            ],
            compiler_params=pltpu.CompilerParams(
                collective_id=0, has_side_effects=True, vmem_limit_bytes=60 * 2**20
            ),
        )(
            tile_index.T, tile_count.T, tile_index.T, tile_count.T, source_points, target_points.T,
            source_mass.reshape(-1, 128), target_mass.reshape(-1, 128),
        )
        return (f * LN2).reshape(-1), (g * LN2).reshape(-1)

    placed = (P("row", None), P("col", "row"), P("row"), P("col"), P("row", "col"), P("row", "col"))
    return jax.shard_map(
        on_device, mesh=mesh, in_specs=placed, out_specs=(P("row"), P("col")), check_vma=False
    )


def solution(mesh):
    return build(mesh, (True,) * 5)
```

```python
import functools
import math

import jax
import jax.numpy as jnp
from jax import lax
from jax.experimental import pallas as pl
from jax.experimental.pallas import tpu as pltpu
from jax.sharding import PartitionSpec as P

TILE = 256
ITERS = 3
LOG2E = 1.4426950408889634
LN2 = 0.6931471805599453
NEG = -1e30
MESH = pl.DeviceIdType.MESH
HALF = 2048
QUART = 1024


def log2(v):
    return jnp.log(v) * LOG2E


def kernel(
    nx, ny, ncol, parts,
    ti_hbm, tc_hbm, sp, tp, sm_hbm, tm_hbm, f_out, g_out,
    ti, tc, tv, cv, sm, tm, X, T0, T1, T2, T3, S, SP, MA, MC, RT, MS, QS, M8, W8, FV, GV, UV, RC, RR, IV,
    lsem, gs, gr, cr, rs, es,
):
    T = (T0, T1, T2, T3)
    row = lax.axis_index("row")
    col = lax.axis_index("col")
    nrow = nx * ny
    x, y = row // ny, lax.rem(row, ny)

    def at(dx, dy):
        return (lax.rem(x + dx + nx, nx) * ny + lax.rem(y + dy + ny, ny), col)

    def row_peer(k):
        return (lax.rem(row + k, nrow), col)

    def col_peer(k):
        return (row, lax.rem(col + k, ncol))

    tables = [
        pltpu.make_async_copy(a, b, lsem.at[2 + k])
        for k, (a, b) in enumerate(
            ((ti_hbm, ti), (tc_hbm, tc), (ti_hbm, tv), (tc_hbm, cv), (sm_hbm, sm), (tm_hbm, tm))
        )
    ]
    for c in tables:
        c.start()
    load_x = pltpu.make_async_copy(sp, X, lsem.at[0])
    load_x.start()

    barrier = pltpu.get_barrier_semaphore()
    for k in range(1, nrow):
        pl.semaphore_signal(barrier, inc=1, device_id=row_peer(k), device_id_type=MESH)
    for k in range(1, ncol):
        pl.semaphore_signal(barrier, inc=1, device_id=col_peer(k), device_id_type=MESH)
    pl.semaphore_wait(barrier, nrow + ncol - 2)

    used = []

    def rows(dy):
        return pl.ds(pl.multiple_of(lax.rem(y + dy + ny, ny) * 64, 64), 64)

    steps = {0: (1, 0), 1: (-1, 0), 2: (0, 1), 3: (0, -1)}

    def fresh():
        used.append(0)
        return len(used) - 1

    def send(src, dst, link, k=None):
        k = fresh() if k is None else k
        c = pltpu.make_async_remote_copy(
            src_ref=src, dst_ref=dst, send_sem=gs.at[link], recv_sem=gr.at[k],
            device_id=at(*steps[link]), device_id_type=MESH,
        )
        c.start()
        return c

    A, B = pl.ds(0, HALF), pl.ds(HALF, HALF)
    A0, A1 = pl.ds(0, QUART), pl.ds(QUART, QUART)
    B0, B1 = pl.ds(HALF, QUART), pl.ds(HALF + QUART, QUART)

    def own(part):
        return tp.at[:, part]

    def along_y(src, d, part, dy):
        return tuple(send(src, T[d].at[rows(dy), part], link) for link in (2, 3))

    def along_x(src, part, dy):
        return (
            send(src, T[3].at[rows(dy), part], 0),
            send(src, T[1].at[rows(dy), part], 1),
        )

    def forward_y(pair, d, low, high):
        k = fresh()
        pair[0].wait_recv()
        send(T[d].at[rows(-1), low], T[d].at[rows(-1), low], 2, k)
        pair[1].wait_recv()
        send(T[d].at[rows(1), high], T[d].at[rows(1), high], 3, k)
        return k

    def forward_x(pair, dy, low, high):
        k = fresh()
        pair[0].wait_recv()
        send(T[3].at[rows(dy), low], T[2].at[rows(dy), low], 0, k)
        pair[1].wait_recv()
        send(T[1].at[rows(dy), high], T[2].at[rows(dy), high], 1, k)
        return k

    def done(*sems):
        for k in sems:
            whole = T[0].at[rows(0), A]
            pltpu.make_async_copy(whole, whole, gr.at[k]).wait()

    scale = LOG2E / math.sqrt(sp.shape[1])
    wide = (32, 8, 128)

    def fold(op, v):
        v = v.reshape((v.shape[0] // 4, 4) + v.shape[1:])
        v = functools.reduce(op, [v[k] for k in range(v.shape[0])])
        while v.shape[0] > 1:
            n = v.shape[0] // 2
            v = op(v[:n], v[n:])
        return v[0]

    def product(chunks, t, s):
        here = pl.ds(pl.multiple_of(t * TILE, TILE), TILE)
        left = [X[here, pl.ds(pl.multiple_of(lax.rem(x + d, nx) * 256, 256), 256)] for d in chunks]
        right = [T[d][:, pl.ds(ti[s, t] * TILE, TILE)] for d in chunks]
        return jnp.dot(
            jnp.concatenate(left, axis=1), jnp.concatenate(right, axis=0), preferred_element_type=jnp.float32
        ) * scale

    def scores(*chunks):
        def body(t, carry):
            for s in range(2):
                p = s * 16 + t
                new = product(chunks, t, s)
                SP[p] = new if chunks == (0,) else SP[p] + new
            return carry

        lax.fori_loop(0, 16, body, 0)

    def idle(t):
        return (tc[0, t].astype(jnp.float32) - 2.0) * 1e30

    if parts[0]:
        a1 = along_x(own(A), A, 0)
        b1 = along_y(own(B), 0, B, 0)
        ay0 = along_y(own(A), 0, A, 0)
        bx0 = along_x(own(B), B, 0)
    keep = pltpu.make_async_copy(tp, T[0].at[rows(0), :], lsem.at[1])
    keep.start()

    for c in tables:
        c.wait()
    small = lax.broadcasted_iota(jnp.int32, (16, 16), 0) == lax.broadcasted_iota(jnp.int32, (16, 16), 1)
    for s in range(2):
        name = jnp.where(cv[...] > s, tv[s:s + 1, :], -1).astype(jnp.float32)
        down = jnp.sum(jnp.where(small, jnp.broadcast_to(name, (16, 16)), 0.0), axis=1, keepdims=True)
        IV[s * 16:(s + 1) * 16, :] = jnp.broadcast_to(down, (16, 128))

    if parts[0]:
        a2 = forward_x(a1, 0, A0, A1)
        ay3 = along_y(T[3].at[rows(0), A], 3, A, 0)
        ay1 = along_y(T[1].at[rows(0), A], 1, A, 0)
        b2 = forward_y(b1, 0, B0, B1)
        bx3 = along_x(T[0].at[rows(-1), B], B, -1)
        bx1 = along_x(T[0].at[rows(1), B], B, 1)
        fay0 = forward_y(ay0, 0, A0, A1)
        fbx0 = forward_x(bx0, 0, B0, B1)
        done(a2)
        ay2 = along_y(T[2].at[rows(0), A], 2, A, 0)
        done(b2)
        bx2 = along_x(T[0].at[rows(2), B], B, 2)
        done(fay0)
    keep.wait()
    load_x.wait()
    if parts[1]:
        scores(0)
    if parts[0]:
        fay3 = forward_y(ay3, 3, A0, A1)
        fay1 = forward_y(ay1, 1, A0, A1)
        fbx3 = forward_x(bx3, -1, B0, B1)
        fbx1 = forward_x(bx1, 1, B0, B1)
        fay2 = forward_y(ay2, 2, A0, A1)
        fbx2 = forward_x(bx2, 2, B0, B1)
        done(fay3, fay1)
    if parts[1]:
        scores(3, 1)
    if parts[0]:
        done(fbx0, fbx3, fbx1, fay2, fbx2)

    def give(buf, it, part, me, n, peer, rsem):
        for k in range(1, n):
            pltpu.make_async_remote_copy(
                src_ref=buf.at[it, part, me], dst_ref=buf.at[it, part, me],
                send_sem=es.at[0], recv_sem=rsem.at[it, part],
                device_id=peer(k), device_id_type=MESH,
            ).start()

    def take(buf, it, part, n, rsem):
        others = buf.at[it, part, pl.ds(0, n - 1)]
        pltpu.make_async_copy(others, others, rsem.at[it, part]).wait()

    def give_rows(it, half):
        if parts[3]:
            give(RC, it, half, col, ncol, col_peer, cr)

    def take_rows(it, half):
        if parts[3]:
            take(RC, it, half, ncol, cr)

    def give_columns(it, h):
        if parts[4]:
            give(RR, it, h, row, nrow, row_peer, rs)

    def take_columns(it, h):
        if parts[4]:
            take(RR, it, h, nrow, rs)

    def log_rows(half):
        eight = slice(half * 8, half * 8 + 8)
        for h in range(2):
            RC[0, half, col, h] = MS[h, eight] + log2(QS[h, eight])
        give_rows(0, half)

    def over_lanes(op, v):
        v = fold(op, v.T.reshape(16, 8, 128))
        n = 8
        while n > 1:
            n //= 2
            v = op(v[:n], v[n:])
        return v

    def as_column(v):
        return jnp.broadcast_to(v, (128, 128)).T

    def finish(t, to):
        r = []
        for s in range(2):
            p = s * 16 + t
            both = SP[p] + product((2,), t, s)
            if s:
                both = both + idle(t)
            for h in range(2):
                S[h, p] = both[:, h * 128:(h + 1) * 128]
                r.append(both[:, h * 128:(h + 1) * 128])
        top = jnp.maximum(jnp.maximum(r[0], r[1]), jnp.maximum(r[2], r[3]))
        e = [jnp.exp2(v - top) for v in r]
        to[...] = top + log2((e[0] + e[1]) + (e[2] + e[3]))

    def row_logs(t, logs):
        for h in range(2):
            v = logs[h * 128:(h + 1) * 128, :].T.reshape(16, 8, 128)
            m8 = fold(jnp.maximum, v)
            s8 = fold(jnp.add, jnp.exp2(v - m8[None]))
            top = jnp.max(m8, axis=0, keepdims=True)
            MS[h, pl.ds(t, 1), :] = top
            QS[h, pl.ds(t, 1), :] = jnp.sum(s8 * jnp.exp2(m8 - top), axis=0, keepdims=True)

    if parts[1]:
        def step(k, carry):
            finish(2 * k + 1, MC)
            row_logs(2 * k, MA)
            finish(2 * k + 2, MA)
            row_logs(2 * k + 1, MC)
            return carry

        finish(0, MA)
        lax.fori_loop(0, 4, step, 0)
    log_rows(0)
    if parts[1]:
        lax.fori_loop(4, 7, step, 0)
        finish(15, MC)
        row_logs(14, MA)
        row_logs(15, MC)
    log_rows(1)

    def spread(t, to):
        for h in range(2):
            to[h * 128:(h + 1) * 128, :] = as_column(UV[h, pl.ds(t, 1), :])

    def each_tile(visit, half, keep):
        spread(8 * half, MA)

        def body(k, carry):
            t = 8 * half + 2 * k
            spread(t + 1, MC)
            visit(t, MA)
            if keep:
                RT[t] = MA[...]
            spread(lax.min(t + 2, 15), MA)
            visit(t + 1, MC)
            if keep:
                RT[t + 1] = MC[...]
            return carry

        lax.fori_loop(0, 4, body, 0)

    def each_kept(visit):
        def body(k, carry):
            visit(8 + k, RT.at[8 + k])
            return carry

        lax.fori_loop(0, 8, body, 0, unroll=2)

    def block(p, h):
        return S[h, p].reshape(wide)

    def column_logs(t, by, lanes):
        add = by[...].reshape(wide)
        for s in range(2):
            p = s * 16 + t
            for h in lanes:
                c = block(p, h) + add
                m8 = fold(jnp.maximum, c)
                e = jnp.exp2(c - m8[None])
                S[h, p] = e.reshape(TILE, 128)
                M8[h, p] = m8
                s8 = fold(jnp.add, e)
                top = jnp.max(m8, axis=0, keepdims=True)
                MS[h, pl.ds(p, 1), :] = top
                QS[h, pl.ds(p, 1), :] = jnp.sum(s8 * jnp.exp2(m8 - top), axis=0, keepdims=True)

    def row_parts():
        def step(t, carry):
            e = [block(s * 16 + t, 0) * W8[0, s * 16 + t][None] for s in range(2)]
            RT[t] = (e[0] + e[1]).reshape(TILE, 128)
            return carry

        lax.fori_loop(0, 16, step, 0, unroll=2)

    def row_sums(it, half):
        def step(k, carry):
            t = 8 * half + k
            e = [block(s * 16 + t, 1) * W8[1, s * 16 + t][None] for s in range(2)]
            total = RT[t] + (e[0] + e[1]).reshape(TILE, 128)
            for h in range(2):
                RC[it, half, col, h, pl.ds(k, 1), :] = over_lanes(jnp.add, total[h * 128:(h + 1) * 128])
            return carry

        lax.fori_loop(0, 8, step, 0, unroll=2)
        give_rows(it, half)

    def column_sums(t, by, lanes):
        by = by[...].reshape(wide)
        for s in range(2):
            p = s * 16 + t
            for h in lanes:
                s8 = fold(jnp.add, block(p, h) * by) * W8[h, p]
                QS[h, pl.ds(p, 1), :] = jnp.sum(s8, axis=0, keepdims=True)

    def merged(got):
        top = jnp.max(got, axis=0)
        return top + log2(jnp.sum(jnp.exp2(got - top[None]), axis=0))

    def mass(ref, h, half):
        return ref[pl.ds(16 * half + h, 8, stride=2), :]

    def all_mass(ref, h):
        return ref[pl.ds(h, 16, stride=2), :]

    def columns(it, visit, combine, ready):
        ready(0)
        if parts[2]:
            each_tile(functools.partial(visit, lanes=(0, 1)), 0, False)
        ready(1)
        for h in range(2):
            if parts[2] and h == 0:
                each_tile(functools.partial(visit, lanes=(h,)), 1, True)
            elif parts[2]:
                each_kept(functools.partial(visit, lanes=(h,)))
            combine(h)
            give_columns(it, h)

    def first_rows(half):
        take_rows(0, half)
        eight = slice(half * 8, half * 8 + 8)
        for h in range(2):
            f = log2(mass(sm, h, half)) - merged(RC[0, half, :, h])
            FV[h, eight] = f
            UV[h, eight] = f

    def first_columns(h):
        one = MS[h] + log2(QS[h])
        for u in range(16):
            named = IV[...] == float(u)
            top = jnp.max(jnp.where(named, one, NEG), axis=0, keepdims=True)
            total = jnp.sum(jnp.where(named, jnp.exp2(one - top), 0.0), axis=0, keepdims=True)
            RR[0, h, row, pl.ds(u, 1), :] = top + log2(jnp.maximum(total, 1e-30))

    columns(0, column_logs, first_columns, first_rows)

    def weigh(first, h):
        def body(t, carry):
            for s in range(2):
                p = s * 16 + t
                if first:
                    g = GV[h, pl.ds(ti[s, t], 1), :]
                    W8[h, p] = jnp.exp2(M8[h, p] + (g if s == 0 else g + idle(t)))
                else:
                    W8[h, p] = W8[h, p] * UV[h, pl.ds(ti[s, t], 1), :]
            return carry

        lax.fori_loop(0, 16, body, 0, unroll=8)

    def columns_arrive(it, h):
        take_columns(it, h)
        if it == 0:
            GV[h] = log2(all_mass(tm, h)) - merged(RR[0, h])
        else:
            v = all_mass(tm, h) / jnp.sum(RR[it, h], axis=0)
            UV[h] = v
            GV[h] = GV[h] + log2(v)

    for it in range(1, ITERS):
        for h in range(2):
            columns_arrive(it - 1, h)
            if parts[2]:
                weigh(it == 1, h)
                if h == 0:
                    row_parts()
        for half in range(2):
            if parts[2]:
                row_sums(it, half)
            else:
                give_rows(it, half)

        def rows_arrive(half, it=it):
            take_rows(it, half)
            eight = slice(half * 8, half * 8 + 8)
            for h in range(2):
                u = mass(sm, h, half) / jnp.sum(RC[it, half, :, h], axis=0)
                UV[h, eight] = u
                if it == ITERS - 1:
                    f_out[pl.ds(16 * half + h, 8, stride=2), :] = FV[h, eight] + log2(u)

        def sum_columns(h, it=it):
            one = QS[h]
            for u in range(16):
                named = IV[...] == float(u)
                RR[it, h, row, pl.ds(u, 1), :] = jnp.sum(jnp.where(named, one, 0.0), axis=0, keepdims=True)

        columns(it, column_sums, sum_columns, rows_arrive)

    for h in range(2):
        columns_arrive(ITERS - 1, h)
        g_out[pl.ds(h, 16, stride=2), :] = GV[h]

    if parts[0]:
        for link in range(4):
            quarter = X.at[pl.ds(0, 960)]
            pltpu.make_async_copy(quarter, quarter, gs.at[link]).wait()
    if parts[3] and parts[4]:
        sent = X.at[pl.ds(0, 8 * ITERS * (nrow + ncol - 2))]
        pltpu.make_async_copy(sent, sent, es.at[0]).wait()


def build(mesh, parts):
    ncol = mesh.shape["col"]
    nrow = mesh.shape["row"]
    nx = ny = math.isqrt(nrow)

    def on_device(source_points, target_points, source_mass, target_mass, tile_index, tile_count):
        n, d = source_points.shape
        m = target_points.shape[0]
        vmem = pl.BlockSpec(memory_space=pltpu.VMEM)
        hbm = pl.BlockSpec(memory_space=pl.ANY)
        f32 = jnp.float32
        f, g = pl.pallas_call(
            functools.partial(kernel, nx, ny, ncol, parts),
            out_shape=(
                jax.ShapeDtypeStruct((n // 128, 128), f32),
                jax.ShapeDtypeStruct((m // 128, 128), f32),
            ),
            in_specs=[hbm] * 6,
            out_specs=(vmem, vmem),
            scratch_shapes=[
                pltpu.SMEM(tile_index.shape[::-1], jnp.int32),
                pltpu.SMEM(tile_count.shape[::-1], jnp.int32),
                pltpu.VMEM(tile_index.shape[::-1], jnp.int32),
                pltpu.VMEM(tile_count.shape[::-1], jnp.int32),
                pltpu.VMEM((n // 128, 128), f32),
                pltpu.VMEM((m // 128, 128), f32),
                pltpu.VMEM((n, d), jnp.bfloat16),
                *[pltpu.VMEM((256, m), jnp.bfloat16) for _ in range(4)],
                pltpu.VMEM((2, 32, TILE, 128), f32),
                pltpu.VMEM((32, TILE, TILE), f32),
                pltpu.VMEM((TILE, 128), f32),
                pltpu.VMEM((TILE, 128), f32),
                pltpu.VMEM((16, TILE, 128), f32),
                pltpu.VMEM((2, 32, 128), f32),
                pltpu.VMEM((2, 32, 128), f32),
                pltpu.VMEM((2, 32, 8, 128), f32),
                pltpu.VMEM((2, 32, 8, 128), f32),
                pltpu.VMEM((2, 16, 128), f32),
                pltpu.VMEM((2, 16, 128), f32),
                pltpu.VMEM((2, 16, 128), f32),
                pltpu.VMEM((ITERS, 2, ncol, 2, 8, 128), f32),
                pltpu.VMEM((ITERS, 2, nrow, 16, 128), f32),
                pltpu.VMEM((32, 128), f32),
                pltpu.SemaphoreType.DMA((8,)),
                pltpu.SemaphoreType.DMA((4,)),
                pltpu.SemaphoreType.DMA((30,)),
                pltpu.SemaphoreType.DMA((ITERS, 2)),
                pltpu.SemaphoreType.DMA((ITERS, 2)),
                pltpu.SemaphoreType.DMA((1,)),
            ],
            compiler_params=pltpu.CompilerParams(
                collective_id=0, has_side_effects=True, vmem_limit_bytes=60 * 2**20
            ),
        )(
            tile_index.T, tile_count.T, source_points, target_points.T,
            source_mass.reshape(-1, 128), target_mass.reshape(-1, 128),
        )
        return (f * LN2).reshape(-1), (g * LN2).reshape(-1)

    placed = (P("row", None), P("col", "row"), P("row"), P("col"), P("row", "col"), P("row", "col"))
    return jax.shard_map(
        on_device, mesh=mesh, in_specs=placed, out_specs=(P("row"), P("col")), check_vma=False
    )


def solution(mesh):
    return build(mesh, (True,) * 5)
```

```python
import functools
import math

import jax
import jax.numpy as jnp
from jax import lax
from jax.experimental import pallas as pl
from jax.experimental.pallas import tpu as pltpu
from jax.sharding import PartitionSpec as P

TILE = 256
ITERS = 3
LOG2E = 1.4426950408889634
LN2 = 0.6931471805599453
NEG = -1e30
MESH = pl.DeviceIdType.MESH
HALF = 16
QUART = 8
SHORT = True


def log2(v):
    return jnp.log(v) * LOG2E


def kernel(
    nx, ny, ncol, parts,
    ti_hbm, tc_hbm, sp, tp, sm_hbm, tm_hbm, f_out, g_out,
    ti, tc, tv, cv, sm, tm, X, T0, T1, T2, T3, S, SP, KA, KB, MA, MC, RT, MS, QS, M8, W8, FV, GV, UV, RC, RR, IV,
    lsem, gs, gr, cr, rs, es,
):
    T = (T0, T1, T2, T3)
    row = lax.axis_index("row")
    col = lax.axis_index("col")
    nrow = nx * ny
    x, y = row // ny, lax.rem(row, ny)

    def at(dx, dy):
        return (lax.rem(x + dx + nx, nx) * ny + lax.rem(y + dy + ny, ny), col)

    def hops(d, n):
        return min(d, n - d)

    row_steps = sorted(
        ((dx, dy) for dx in range(nx) for dy in range(ny) if dx or dy),
        key=lambda d: -hops(d[0], nx) - hops(d[1], ny),
    )
    row_peers = [at(*d) for d in row_steps]
    z, core = col // 2, lax.rem(col, 2)
    col_steps = sorted(((dz, dc) for dz in range(ncol // 2) for dc in range(2) if dz or dc), key=lambda d: -hops(d[0], ncol // 2))
    col_peers = [(row, lax.rem(z + dz, ncol // 2) * 2 + lax.rem(core + dc, 2)) for dz, dc in col_steps]

    tables = [
        pltpu.make_async_copy(a, b, lsem.at[2 + k])
        for k, (a, b) in enumerate(
            ((ti_hbm, ti), (tc_hbm, tc), (ti_hbm, tv), (tc_hbm, cv), (sm_hbm, sm), (tm_hbm, tm))
        )
    ]
    for c in tables:
        c.start()
    def rows(dy):
        return pl.ds(pl.multiple_of(lax.rem(y + dy + ny, ny) * 64, 64), 64)

    for b in range(32):
        pltpu.make_async_copy(tp.at[:, pl.ds(128 * b, 128)], T[0].at[b, rows(0)], lsem.at[1]).start()

    load_x = [pltpu.make_async_copy(sp.at[:, pl.ds(128 * k, 128)], X.at[k], lsem.at[0]) for k in range(8)]
    for c in load_x:
        c.start()

    barrier = pltpu.get_barrier_semaphore()
    greeted = [at(1, 0), at(-1, 0), at(0, 1), at(0, -1)] + col_peers if SHORT else row_peers + col_peers
    for peer in greeted:
        pl.semaphore_signal(barrier, inc=1, device_id=peer, device_id_type=MESH)
    pl.semaphore_wait(barrier, len(greeted))

    mine = T[0].at[:, rows(0)]
    pltpu.make_async_copy(mine, mine, lsem.at[1]).wait()
    used = []

    steps = {0: (1, 0), 1: (-1, 0), 2: (0, 1), 3: (0, -1)}

    def fresh():
        used.append(0)
        return len(used) - 1

    def send(src, dst, link, k=None):
        k = fresh() if k is None else k
        c = pltpu.make_async_remote_copy(
            src_ref=src, dst_ref=dst, send_sem=gs.at[link], recv_sem=gr.at[k],
            device_id=at(*steps[link]), device_id_type=MESH,
        )
        c.start()
        return c

    A, B = pl.ds(0, HALF), pl.ds(HALF, HALF)
    A0, A1 = pl.ds(0, QUART), pl.ds(QUART, QUART)
    B0, B1 = pl.ds(HALF, QUART), pl.ds(HALF + QUART, QUART)

    def own(part):
        return T[0].at[part, rows(0)]

    def along_y(src, d, part, dy):
        return tuple(send(src, T[d].at[part, rows(dy)], link) for link in (2, 3))

    def along_x(src, part, dy):
        return (
            send(src, T[3].at[part, rows(dy)], 0),
            send(src, T[1].at[part, rows(dy)], 1),
        )

    def forward_y(pair, d, low, high):
        k = fresh()
        pair[0].wait_recv()
        send(T[d].at[low, rows(-1)], T[d].at[low, rows(-1)], 2, k)
        pair[1].wait_recv()
        send(T[d].at[high, rows(1)], T[d].at[high, rows(1)], 3, k)
        return k

    def forward_x(pair, dy, low, high):
        k = fresh()
        pair[0].wait_recv()
        send(T[3].at[low, rows(dy)], T[2].at[low, rows(dy)], 0, k)
        pair[1].wait_recv()
        send(T[1].at[high, rows(dy)], T[2].at[high, rows(dy)], 1, k)
        return k

    def done(*sems):
        for k in sems:
            whole = T[0].at[A, rows(0)]
            pltpu.make_async_copy(whole, whole, gr.at[k]).wait()

    scale = LOG2E / math.sqrt(sp.shape[1])
    wide = (32, 8, 128)

    def fold(op, v):
        v = v.reshape((v.shape[0] // 4, 4) + v.shape[1:])
        v = functools.reduce(op, [v[k] for k in range(v.shape[0])])
        while v.shape[0] > 1:
            n = v.shape[0] // 2
            v = op(v[:n], v[n:])
        return v[0]

    def product(chunks, t, s):
        here = pl.ds(pl.multiple_of(t * TILE, TILE), TILE)
        left = [X[lax.rem(x + d, nx) * 2 + k, here, :] for d in chunks for k in range(2)]
        right = [jnp.concatenate([T[d][ti[s, t] * 2 + k] for k in range(2)], axis=1) for d in chunks]
        return jnp.dot(
            jnp.concatenate(left, axis=1), jnp.concatenate(right, axis=0), preferred_element_type=jnp.float32
        ) * scale

    def scores(*chunks):
        def body(t, carry):
            for s in range(2):
                p = s * 16 + t
                new = product(chunks, t, s)
                SP[p] = new if chunks == (0,) else SP[p] + new
            return carry

        lax.fori_loop(0, 16, body, 0)

    def idle(t):
        return (tc[0, t].astype(jnp.float32) - 2.0) * 1e30

    if parts[0]:
        a1 = along_x(own(A), A, 0)
        b1 = along_y(own(B), 0, B, 0)
        ay0 = along_y(own(A), 0, A, 0)
        bx0 = along_x(own(B), B, 0)

    for c in tables:
        c.wait()
    small = lax.broadcasted_iota(jnp.int32, (16, 16), 0) == lax.broadcasted_iota(jnp.int32, (16, 16), 1)
    for s in range(2):
        name = jnp.where(cv[...] > s, tv[s:s + 1, :], -1).astype(jnp.float32)
        down = jnp.sum(jnp.where(small, jnp.broadcast_to(name, (16, 16)), 0.0), axis=1, keepdims=True)
        IV[s * 16:(s + 1) * 16, :] = jnp.broadcast_to(down, (16, 128))

    if parts[0]:
        a2 = forward_x(a1, 0, A0, A1)
        ay3 = along_y(T[3].at[A, rows(0)], 3, A, 0)
        ay1 = along_y(T[1].at[A, rows(0)], 1, A, 0)
        b2 = forward_y(b1, 0, B0, B1)
        bx3 = along_x(T[0].at[B, rows(-1)], B, -1)
        bx1 = along_x(T[0].at[B, rows(1)], B, 1)
        fay0 = forward_y(ay0, 0, A0, A1)
        fbx0 = forward_x(bx0, 0, B0, B1)
        done(a2)
        ay2 = along_y(T[2].at[A, rows(0)], 2, A, 0)
        done(b2)
        bx2 = along_x(T[0].at[B, rows(2)], B, 2)
        done(fay0)
    pltpu.make_async_copy(X, X, lsem.at[0]).wait()
    if parts[1]:
        scores(0)
    if parts[0]:
        fay3 = forward_y(ay3, 3, A0, A1)
        fay1 = forward_y(ay1, 1, A0, A1)
        fbx3 = forward_x(bx3, -1, B0, B1)
        fbx1 = forward_x(bx1, 1, B0, B1)
        fay2 = forward_y(ay2, 2, A0, A1)
        fbx2 = forward_x(bx2, 2, B0, B1)
        done(fay3, fay1)
    if parts[1]:
        scores(3, 1)
    if parts[0]:
        done(fbx0, fbx3, fbx1, fay2, fbx2)

    def give(buf, it, part, me, peers, rsem):
        for peer in peers:
            pltpu.make_async_remote_copy(
                src_ref=buf.at[it, part, me], dst_ref=buf.at[it, part, me],
                send_sem=es.at[0], recv_sem=rsem.at[it, part],
                device_id=peer, device_id_type=MESH,
            ).start()

    def take(buf, it, part, n, rsem):
        others = buf.at[it, part, pl.ds(0, n - 1)]
        pltpu.make_async_copy(others, others, rsem.at[it, part]).wait()

    def give_rows(it, half):
        if parts[3]:
            give(RC, it, half, col, col_peers, cr)

    def take_rows(it, half):
        if parts[3]:
            take(RC, it, half, ncol, cr)

    def give_columns(it, h):
        if parts[4]:
            give(RR, it, h, row, row_peers, rs)

    def take_columns(it, h):
        if parts[4]:
            take(RR, it, h, nrow, rs)

    def log_rows(half):
        eight = slice(half * 8, half * 8 + 8)
        for h in range(2):
            RC[0, half, col, h] = MS[h, eight] + log2(QS[h, eight])
        give_rows(0, half)

    def over_lanes(op, v):
        v = fold(op, v.T.reshape(16, 8, 128))
        n = 8
        while n > 1:
            n //= 2
            v = op(v[:n], v[n:])
        return v

    def as_column(v):
        return jnp.broadcast_to(v, (128, 128)).T

    def finish(t, K):
        for s in range(2):
            p = s * 16 + t
            both = SP[p] + product((2,), t, s)
            if s:
                both = both + idle(t)
            for h in range(2):
                S[h, p] = both[:, h * 128:(h + 1) * 128]
                K[s, h] = both[:, h * 128:(h + 1) * 128]

    def lane_logs(K, to):
        r = [K[s, h] for s in range(2) for h in range(2)]
        top = jnp.maximum(jnp.maximum(r[0], r[1]), jnp.maximum(r[2], r[3]))
        e = [jnp.exp2(v - top) for v in r]
        to[...] = top + log2((e[0] + e[1]) + (e[2] + e[3]))

    def row_logs(t, logs):
        for h in range(2):
            v = logs[h * 128:(h + 1) * 128, :].T.reshape(16, 8, 128)
            m8 = fold(jnp.maximum, v)
            s8 = fold(jnp.add, jnp.exp2(v - m8[None]))
            top = jnp.max(m8, axis=0, keepdims=True)
            MS[h, pl.ds(t, 1), :] = top
            QS[h, pl.ds(t, 1), :] = jnp.sum(s8 * jnp.exp2(m8 - top), axis=0, keepdims=True)

    if parts[1]:
        def stages(t, now):
            if 2 in now:
                row_logs(t - 2, MA)
            if 1 in now:
                lane_logs(KA, MA)
            if 0 in now:
                finish(t, KA)

        def step(t, carry):
            stages(t, (2, 1, 0))
            return carry

        stages(0, (0,))
        stages(1, (1, 0))
        lax.fori_loop(2, 10, step, 0)
    log_rows(0)
    if parts[1]:
        lax.fori_loop(10, 16, step, 0)
        stages(16, (2, 1))
        stages(17, (2,))
    log_rows(1)

    def spread(t, to):
        for h in range(2):
            to[h * 128:(h + 1) * 128, :] = as_column(UV[h, pl.ds(t, 1), :])

    def each_tile(visit, half, keep):
        spread(8 * half, MA)

        def body(k, carry):
            t = 8 * half + 2 * k
            spread(t + 1, MC)
            visit(t, MA)
            if keep:
                RT[t] = MA[...]
            spread(lax.min(t + 2, 15), MA)
            visit(t + 1, MC)
            if keep:
                RT[t + 1] = MC[...]
            return carry

        lax.fori_loop(0, 4, body, 0)

    def each_kept(visit):
        def body(k, carry):
            visit(8 + k, RT.at[8 + k])
            return carry

        lax.fori_loop(0, 8, body, 0, unroll=2)

    def block(p, h):
        return S[h, p].reshape(wide)

    def column_logs(t, by, lanes):
        add = by[...].reshape(wide)
        for s in range(2):
            p = s * 16 + t
            for h in lanes:
                c = block(p, h) + add
                m8 = fold(jnp.maximum, c)
                e = jnp.exp2(c - m8[None])
                S[h, p] = e.reshape(TILE, 128)
                M8[h, p] = m8
                s8 = fold(jnp.add, e)
                top = jnp.max(m8, axis=0, keepdims=True)
                MS[h, pl.ds(p, 1), :] = top
                QS[h, pl.ds(p, 1), :] = jnp.sum(s8 * jnp.exp2(m8 - top), axis=0, keepdims=True)

    def row_parts():
        def step(t, carry):
            e = [block(s * 16 + t, 0) * W8[0, s * 16 + t][None] for s in range(2)]
            RT[t] = (e[0] + e[1]).reshape(TILE, 128)
            return carry

        lax.fori_loop(0, 16, step, 0, unroll=2)

    def row_sums(it, half):
        def step(k, carry):
            t = 8 * half + k
            e = [block(s * 16 + t, 1) * W8[1, s * 16 + t][None] for s in range(2)]
            total = RT[t] + (e[0] + e[1]).reshape(TILE, 128)
            for h in range(2):
                RC[it, half, col, h, pl.ds(k, 1), :] = over_lanes(jnp.add, total[h * 128:(h + 1) * 128])
            return carry

        lax.fori_loop(0, 8, step, 0, unroll=2)
        give_rows(it, half)

    def column_sums(t, by, lanes):
        by = by[...].reshape(wide)
        for s in range(2):
            p = s * 16 + t
            for h in lanes:
                s8 = fold(jnp.add, block(p, h) * by) * W8[h, p]
                QS[h, pl.ds(p, 1), :] = jnp.sum(s8, axis=0, keepdims=True)

    def merged(got):
        top = jnp.max(got, axis=0)
        return top + log2(jnp.sum(jnp.exp2(got - top[None]), axis=0))

    def mass(ref, h, half):
        return ref[pl.ds(16 * half + h, 8, stride=2), :]

    def all_mass(ref, h):
        return ref[pl.ds(h, 16, stride=2), :]

    def columns(it, visit, combine, ready):
        ready(0)
        if parts[2]:
            each_tile(functools.partial(visit, lanes=(0, 1)), 0, False)
        ready(1)
        for h in range(2):
            if parts[2] and h == 0:
                each_tile(functools.partial(visit, lanes=(h,)), 1, True)
            elif parts[2]:
                each_kept(functools.partial(visit, lanes=(h,)))
            combine(h)
            give_columns(it, h)

    def first_rows(half):
        take_rows(0, half)
        eight = slice(half * 8, half * 8 + 8)
        for h in range(2):
            f = log2(mass(sm, h, half)) - merged(RC[0, half, :, h])
            FV[h, eight] = f
            UV[h, eight] = f

    def first_columns(h):
        one = MS[h] + log2(QS[h])
        for u in range(16):
            named = IV[...] == float(u)
            top = jnp.max(jnp.where(named, one, NEG), axis=0, keepdims=True)
            total = jnp.sum(jnp.where(named, jnp.exp2(one - top), 0.0), axis=0, keepdims=True)
            RR[0, h, row, pl.ds(u, 1), :] = top + log2(jnp.maximum(total, 1e-30))

    columns(0, column_logs, first_columns, first_rows)

    def weigh(first, h):
        def body(t, carry):
            for s in range(2):
                p = s * 16 + t
                if first:
                    g = GV[h, pl.ds(ti[s, t], 1), :]
                    W8[h, p] = jnp.exp2(M8[h, p] + (g if s == 0 else g + idle(t)))
                else:
                    W8[h, p] = W8[h, p] * UV[h, pl.ds(ti[s, t], 1), :]
            return carry

        lax.fori_loop(0, 16, body, 0, unroll=8)

    def columns_arrive(it, h):
        take_columns(it, h)
        if it == 0:
            GV[h] = log2(all_mass(tm, h)) - merged(RR[0, h])
        else:
            v = all_mass(tm, h) / jnp.sum(RR[it, h], axis=0)
            UV[h] = v
            GV[h] = GV[h] + log2(v)

    for it in range(1, ITERS):
        for h in range(2):
            columns_arrive(it - 1, h)
            if parts[2]:
                weigh(it == 1, h)
                if h == 0:
                    row_parts()
        for half in range(2):
            if parts[2]:
                row_sums(it, half)
            else:
                give_rows(it, half)

        def rows_arrive(half, it=it):
            take_rows(it, half)
            eight = slice(half * 8, half * 8 + 8)
            for h in range(2):
                u = mass(sm, h, half) / jnp.sum(RC[it, half, :, h], axis=0)
                UV[h, eight] = u
                if it == ITERS - 1:
                    f_out[pl.ds(16 * half + h, 8, stride=2), :] = FV[h, eight] + log2(u)

        def sum_columns(h, it=it):
            one = QS[h]
            for u in range(16):
                named = IV[...] == float(u)
                RR[it, h, row, pl.ds(u, 1), :] = jnp.sum(jnp.where(named, one, 0.0), axis=0, keepdims=True)

        columns(it, column_sums, sum_columns, rows_arrive)

    for h in range(2):
        columns_arrive(ITERS - 1, h)
        g_out[pl.ds(h, 16, stride=2), :] = GV[h]

    if parts[0]:
        for link in range(4):
            quarter = X.at[pl.ds(0, 2), pl.ds(0, 3840)]
            pltpu.make_async_copy(quarter, quarter, gs.at[link]).wait()
    if parts[3] and parts[4]:
        sent = X.at[pl.ds(0, 2), pl.ds(0, 32 * ITERS * (nrow + ncol - 2))]
        pltpu.make_async_copy(sent, sent, es.at[0]).wait()


def build(mesh, parts):
    ncol = mesh.shape["col"]
    nrow = mesh.shape["row"]
    nx = ny = math.isqrt(nrow)

    def on_device(source_points, target_points, source_mass, target_mass, tile_index, tile_count):
        n, d = source_points.shape
        m = target_points.shape[0]
        vmem = pl.BlockSpec(memory_space=pltpu.VMEM)
        hbm = pl.BlockSpec(memory_space=pl.ANY)
        f32 = jnp.float32
        f, g = pl.pallas_call(
            functools.partial(kernel, nx, ny, ncol, parts),
            out_shape=(
                jax.ShapeDtypeStruct((n // 128, 128), f32),
                jax.ShapeDtypeStruct((m // 128, 128), f32),
            ),
            in_specs=[hbm] * 6,
            out_specs=(vmem, vmem),
            scratch_shapes=[
                pltpu.SMEM(tile_index.shape[::-1], jnp.int32),
                pltpu.SMEM(tile_count.shape[::-1], jnp.int32),
                pltpu.VMEM(tile_index.shape[::-1], jnp.int32),
                pltpu.VMEM(tile_count.shape[::-1], jnp.int32),
                pltpu.VMEM((n // 128, 128), f32),
                pltpu.VMEM((m // 128, 128), f32),
                pltpu.VMEM((d // 128, n, 128), jnp.bfloat16),
                *[pltpu.VMEM((m // 128, 256, 128), jnp.bfloat16) for _ in range(4)],
                pltpu.VMEM((2, 32, TILE, 128), f32),
                pltpu.VMEM((32, TILE, TILE), f32),
                pltpu.VMEM((2, 2, TILE, 128), f32),
                pltpu.VMEM((2, 2, TILE, 128), f32),
                pltpu.VMEM((TILE, 128), f32),
                pltpu.VMEM((TILE, 128), f32),
                pltpu.VMEM((16, TILE, 128), f32),
                pltpu.VMEM((2, 32, 128), f32),
                pltpu.VMEM((2, 32, 128), f32),
                pltpu.VMEM((2, 32, 8, 128), f32),
                pltpu.VMEM((2, 32, 8, 128), f32),
                pltpu.VMEM((2, 16, 128), f32),
                pltpu.VMEM((2, 16, 128), f32),
                pltpu.VMEM((2, 16, 128), f32),
                pltpu.VMEM((ITERS, 2, ncol, 2, 8, 128), f32),
                pltpu.VMEM((ITERS, 2, nrow, 16, 128), f32),
                pltpu.VMEM((32, 128), f32),
                pltpu.SemaphoreType.DMA((8,)),
                pltpu.SemaphoreType.DMA((4,)),
                pltpu.SemaphoreType.DMA((30,)),
                pltpu.SemaphoreType.DMA((ITERS, 2)),
                pltpu.SemaphoreType.DMA((ITERS, 2)),
                pltpu.SemaphoreType.DMA((1,)),
            ],
            compiler_params=pltpu.CompilerParams(
                collective_id=0, has_side_effects=True, vmem_limit_bytes=60 * 2**20
            ),
        )(
            tile_index.T, tile_count.T, source_points, target_points.T,
            source_mass.reshape(-1, 128), target_mass.reshape(-1, 128),
        )
        return (f * LN2).reshape(-1), (g * LN2).reshape(-1)

    placed = (P("row", None), P("col", "row"), P("row"), P("col"), P("row", "col"), P("row", "col"))
    return jax.shard_map(
        on_device, mesh=mesh, in_specs=placed, out_specs=(P("row"), P("col")), check_vma=False
    )


def solution(mesh):
    return build(mesh, (True,) * 5)
```

```python
import functools
import math

import jax
import jax.numpy as jnp
from jax import lax
from jax.experimental import pallas as pl
from jax.experimental.pallas import tpu as pltpu
from jax.sharding import PartitionSpec as P

TILE = 256
ITERS = 3
LOG2E = 1.4426950408889634
LN2 = 0.6931471805599453
NEG = -1e30
MESH = pl.DeviceIdType.MESH
HALF = 16
QUART = 8
SHORT = True


def log2(v):
    return jnp.log(v) * LOG2E


def kernel(
    nx, ny, ncol, parts,
    ti_hbm, tc_hbm, sp, tp, sm_hbm, tm_hbm, f_out, g_out,
    ti, tc, tv, cv, sm, tm, X, T0, T1, T2, T3, S, SP, KA, KB, MA, MC, RT, MS, QS, M8, W8, FV, GV, UV, RC, RR, IV,
    lsem, gs, gr, cr, rs, es,
):
    T = (T0, T1, T2, T3)
    row = lax.axis_index("row")
    col = lax.axis_index("col")
    nrow = nx * ny
    x, y = row // ny, lax.rem(row, ny)

    def at(dx, dy):
        return (lax.rem(x + dx + nx, nx) * ny + lax.rem(y + dy + ny, ny), col)

    def hops(d, n):
        return min(d, n - d)

    row_steps = sorted(
        ((dx, dy) for dx in range(nx) for dy in range(ny) if dx or dy),
        key=lambda d: -hops(d[0], nx) - hops(d[1], ny),
    )
    row_peers = [at(*d) for d in row_steps]
    z, core = col // 2, lax.rem(col, 2)
    col_steps = sorted(((dz, dc) for dz in range(ncol // 2) for dc in range(2) if dz or dc), key=lambda d: -hops(d[0], ncol // 2))
    col_peers = [(row, lax.rem(z + dz, ncol // 2) * 2 + lax.rem(core + dc, 2)) for dz, dc in col_steps]

    barrier = pltpu.get_barrier_semaphore()
    greeted = [at(1, 0), at(-1, 0), at(0, 1), at(0, -1)] + col_peers if SHORT else row_peers + col_peers
    for peer in greeted:
        pl.semaphore_signal(barrier, inc=1, device_id=peer, device_id_type=MESH)
    def rows(dy):
        return pl.ds(pl.multiple_of(lax.rem(y + dy + ny, ny) * 64, 64), 64)

    for b in range(32):
        pltpu.make_async_copy(tp.at[:, pl.ds(128 * b, 128)], T[0].at[b, rows(0)], lsem.at[1]).start()

    pl.semaphore_wait(barrier, len(greeted))

    mine = T[0].at[:, rows(0)]
    pltpu.make_async_copy(mine, mine, lsem.at[1]).wait()
    used = []

    steps = {0: (1, 0), 1: (-1, 0), 2: (0, 1), 3: (0, -1)}

    def fresh():
        used.append(0)
        return len(used) - 1

    def send(src, dst, link, k=None):
        k = fresh() if k is None else k
        c = pltpu.make_async_remote_copy(
            src_ref=src, dst_ref=dst, send_sem=gs.at[link], recv_sem=gr.at[k],
            device_id=at(*steps[link]), device_id_type=MESH,
        )
        c.start()
        return c

    A, B = pl.ds(0, HALF), pl.ds(HALF, HALF)
    A0, A1 = pl.ds(0, QUART), pl.ds(QUART, QUART)
    B0, B1 = pl.ds(HALF, QUART), pl.ds(HALF + QUART, QUART)

    def own(part):
        return T[0].at[part, rows(0)]

    def along_y(src, d, part, dy):
        return tuple(send(src, T[d].at[part, rows(dy)], link) for link in (2, 3))

    def along_x(src, part, dy):
        return (
            send(src, T[3].at[part, rows(dy)], 0),
            send(src, T[1].at[part, rows(dy)], 1),
        )

    def forward_y(pair, d, low, high):
        k = fresh()
        pair[0].wait_recv()
        send(T[d].at[low, rows(-1)], T[d].at[low, rows(-1)], 2, k)
        pair[1].wait_recv()
        send(T[d].at[high, rows(1)], T[d].at[high, rows(1)], 3, k)
        return k

    def forward_x(pair, dy, low, high):
        k = fresh()
        pair[0].wait_recv()
        send(T[3].at[low, rows(dy)], T[2].at[low, rows(dy)], 0, k)
        pair[1].wait_recv()
        send(T[1].at[high, rows(dy)], T[2].at[high, rows(dy)], 1, k)
        return k

    def done(*sems):
        for k in sems:
            whole = T[0].at[A, rows(0)]
            pltpu.make_async_copy(whole, whole, gr.at[k]).wait()

    scale = LOG2E / math.sqrt(sp.shape[1])
    wide = (32, 8, 128)

    def fold(op, v):
        v = v.reshape((v.shape[0] // 4, 4) + v.shape[1:])
        v = functools.reduce(op, [v[k] for k in range(v.shape[0])])
        while v.shape[0] > 1:
            n = v.shape[0] // 2
            v = op(v[:n], v[n:])
        return v[0]

    def product(chunks, t, s):
        here = pl.ds(pl.multiple_of(t * TILE, TILE), TILE)
        left = [X[lax.rem(x + d, nx) * 2 + k, here, :] for d in chunks for k in range(2)]
        right = [jnp.concatenate([T[d][ti[s, t] * 2 + k] for k in range(2)], axis=1) for d in chunks]
        return jnp.dot(
            jnp.concatenate(left, axis=1), jnp.concatenate(right, axis=0), preferred_element_type=jnp.float32
        ) * scale

    def scores(*chunks):
        def body(t, carry):
            for s in range(2):
                p = s * 16 + t
                new = product(chunks, t, s)
                SP[p] = new if chunks == (0,) else SP[p] + new
            return carry

        lax.fori_loop(0, 16, body, 0)

    def idle(t):
        return (tc[0, t].astype(jnp.float32) - 2.0) * 1e30

    if parts[0]:
        a1 = along_x(own(A), A, 0)
        b1 = along_y(own(B), 0, B, 0)
        ay0 = along_y(own(A), 0, A, 0)
        bx0 = along_x(own(B), B, 0)

    tables = [
        pltpu.make_async_copy(a, b, lsem.at[2 + k])
        for k, (a, b) in enumerate(
            ((ti_hbm, ti), (tc_hbm, tc), (ti_hbm, tv), (tc_hbm, cv), (sm_hbm, sm), (tm_hbm, tm))
        )
    ]
    for c in tables:
        c.start()
    load_x = [pltpu.make_async_copy(sp.at[:, pl.ds(128 * k, 128)], X.at[k], lsem.at[0]) for k in range(8)]
    for c in load_x:
        c.start()

    for c in tables:
        c.wait()
    small = lax.broadcasted_iota(jnp.int32, (16, 16), 0) == lax.broadcasted_iota(jnp.int32, (16, 16), 1)
    for s in range(2):
        name = jnp.where(cv[...] > s, tv[s:s + 1, :], -1).astype(jnp.float32)
        down = jnp.sum(jnp.where(small, jnp.broadcast_to(name, (16, 16)), 0.0), axis=1, keepdims=True)
        IV[s * 16:(s + 1) * 16, :] = jnp.broadcast_to(down, (16, 128))

    if parts[0]:
        a2 = forward_x(a1, 0, A0, A1)
        ay3 = along_y(T[3].at[A, rows(0)], 3, A, 0)
        ay1 = along_y(T[1].at[A, rows(0)], 1, A, 0)
        b2 = forward_y(b1, 0, B0, B1)
        bx3 = along_x(T[0].at[B, rows(-1)], B, -1)
        bx1 = along_x(T[0].at[B, rows(1)], B, 1)
        fay0 = forward_y(ay0, 0, A0, A1)
        fbx0 = forward_x(bx0, 0, B0, B1)
        done(a2)
        ay2 = along_y(T[2].at[A, rows(0)], 2, A, 0)
        done(b2)
        bx2 = along_x(T[0].at[B, rows(2)], B, 2)
        done(fay0)
    pltpu.make_async_copy(X, X, lsem.at[0]).wait()
    if parts[1]:
        scores(0)
    if parts[0]:
        fay3 = forward_y(ay3, 3, A0, A1)
        fay1 = forward_y(ay1, 1, A0, A1)
        fbx3 = forward_x(bx3, -1, B0, B1)
        fbx1 = forward_x(bx1, 1, B0, B1)
        fay2 = forward_y(ay2, 2, A0, A1)
        fbx2 = forward_x(bx2, 2, B0, B1)
        done(fay3, fay1)
    if parts[1]:
        scores(3, 1)
    if parts[0]:
        done(fbx0, fbx3, fbx1, fay2, fbx2)

    def give(buf, it, part, me, peers, rsem):
        for peer in peers:
            pltpu.make_async_remote_copy(
                src_ref=buf.at[it, part, me], dst_ref=buf.at[it, part, me],
                send_sem=es.at[0], recv_sem=rsem.at[it, part],
                device_id=peer, device_id_type=MESH,
            ).start()

    def take(buf, it, part, n, rsem):
        others = buf.at[it, part, pl.ds(0, n - 1)]
        pltpu.make_async_copy(others, others, rsem.at[it, part]).wait()

    def give_rows(it, half):
        if parts[3]:
            give(RC, it, half, col, col_peers, cr)

    def take_rows(it, half):
        if parts[3]:
            take(RC, it, half, ncol, cr)

    def give_columns(it, h):
        if parts[4]:
            give(RR, it, h, row, row_peers, rs)

    def take_columns(it, h):
        if parts[4]:
            take(RR, it, h, nrow, rs)

    def log_rows(half):
        eight = slice(half * 8, half * 8 + 8)
        for h in range(2):
            RC[0, half, col, h] = MS[h, eight] + log2(QS[h, eight])
        give_rows(0, half)

    def over_lanes(op, v):
        v = fold(op, v.T.reshape(16, 8, 128))
        n = 8
        while n > 1:
            n //= 2
            v = op(v[:n], v[n:])
        return v

    def as_column(v):
        return jnp.broadcast_to(v, (128, 128)).T

    def finish(t, K):
        for s in range(2):
            p = s * 16 + t
            both = SP[p] + product((2,), t, s)
            if s:
                both = both + idle(t)
            for h in range(2):
                S[h, p] = both[:, h * 128:(h + 1) * 128]
                K[s, h] = both[:, h * 128:(h + 1) * 128]

    def lane_logs(K, to):
        r = [K[s, h] for s in range(2) for h in range(2)]
        top = jnp.maximum(jnp.maximum(r[0], r[1]), jnp.maximum(r[2], r[3]))
        e = [jnp.exp2(v - top) for v in r]
        to[...] = top + log2((e[0] + e[1]) + (e[2] + e[3]))

    def row_logs(t, logs):
        for h in range(2):
            v = logs[h * 128:(h + 1) * 128, :].T.reshape(16, 8, 128)
            m8 = fold(jnp.maximum, v)
            s8 = fold(jnp.add, jnp.exp2(v - m8[None]))
            top = jnp.max(m8, axis=0, keepdims=True)
            MS[h, pl.ds(t, 1), :] = top
            QS[h, pl.ds(t, 1), :] = jnp.sum(s8 * jnp.exp2(m8 - top), axis=0, keepdims=True)

    if parts[1]:
        def stages(t, now):
            if 2 in now:
                row_logs(t - 2, MA)
            if 1 in now:
                lane_logs(KA, MA)
            if 0 in now:
                finish(t, KA)

        def step(t, carry):
            stages(t, (2, 1, 0))
            return carry

        stages(0, (0,))
        stages(1, (1, 0))
        lax.fori_loop(2, 10, step, 0)
    log_rows(0)
    if parts[1]:
        lax.fori_loop(10, 16, step, 0)
        stages(16, (2, 1))
        stages(17, (2,))
    log_rows(1)

    def spread(t, to):
        for h in range(2):
            to[h * 128:(h + 1) * 128, :] = as_column(UV[h, pl.ds(t, 1), :])

    def each_tile(visit, half, keep):
        spread(8 * half, MA)

        def body(k, carry):
            t = 8 * half + 2 * k
            spread(t + 1, MC)
            visit(t, MA)
            if keep:
                RT[t] = MA[...]
            spread(lax.min(t + 2, 15), MA)
            visit(t + 1, MC)
            if keep:
                RT[t + 1] = MC[...]
            return carry

        lax.fori_loop(0, 4, body, 0, unroll=2)

    def each_kept(visit):
        def body(k, carry):
            visit(8 + k, RT.at[8 + k])
            return carry

        lax.fori_loop(0, 8, body, 0, unroll=2)

    def block(p, h):
        return S[h, p].reshape(wide)

    def column_logs(t, by, lanes):
        add = by[...].reshape(wide)
        for s in range(2):
            p = s * 16 + t
            for h in lanes:
                c = block(p, h) + add
                m8 = fold(jnp.maximum, c)
                e = jnp.exp2(c - m8[None])
                S[h, p] = e.reshape(TILE, 128)
                M8[h, p] = m8
                s8 = fold(jnp.add, e)
                top = jnp.max(m8, axis=0, keepdims=True)
                MS[h, pl.ds(p, 1), :] = top
                QS[h, pl.ds(p, 1), :] = jnp.sum(s8 * jnp.exp2(m8 - top), axis=0, keepdims=True)

    def row_parts():
        def step(t, carry):
            e = [block(s * 16 + t, 0) * W8[0, s * 16 + t][None] for s in range(2)]
            RT[t] = (e[0] + e[1]).reshape(TILE, 128)
            return carry

        lax.fori_loop(0, 16, step, 0, unroll=2)

    def row_sums(it, half):
        def step(k, carry):
            t = 8 * half + k
            e = [block(s * 16 + t, 1) * W8[1, s * 16 + t][None] for s in range(2)]
            total = RT[t] + (e[0] + e[1]).reshape(TILE, 128)
            for h in range(2):
                RC[it, half, col, h, pl.ds(k, 1), :] = over_lanes(jnp.add, total[h * 128:(h + 1) * 128])
            return carry

        lax.fori_loop(0, 8, step, 0, unroll=8)
        give_rows(it, half)

    def column_sums(t, by, lanes):
        by = by[...].reshape(wide)
        for s in range(2):
            p = s * 16 + t
            for h in lanes:
                s8 = fold(jnp.add, block(p, h) * by) * W8[h, p]
                QS[h, pl.ds(p, 1), :] = jnp.sum(s8, axis=0, keepdims=True)

    def merged(got):
        top = jnp.max(got, axis=0)
        return top + log2(jnp.sum(jnp.exp2(got - top[None]), axis=0))

    def mass(ref, h, half):
        return ref[pl.ds(16 * half + h, 8, stride=2), :]

    def all_mass(ref, h):
        return ref[pl.ds(h, 16, stride=2), :]

    def columns(it, visit, combine, ready):
        ready(0)
        if parts[2]:
            each_tile(functools.partial(visit, lanes=(0, 1)), 0, False)
        ready(1)
        for h in range(2):
            if parts[2] and h == 0:
                each_tile(functools.partial(visit, lanes=(h,)), 1, True)
            elif parts[2]:
                each_kept(functools.partial(visit, lanes=(h,)))
            combine(h)
            give_columns(it, h)

    def first_rows(half):
        take_rows(0, half)
        eight = slice(half * 8, half * 8 + 8)
        for h in range(2):
            f = log2(mass(sm, h, half)) - merged(RC[0, half, :, h])
            FV[h, eight] = f
            UV[h, eight] = f

    def first_columns(h):
        one = MS[h] + log2(QS[h])
        for u in range(16):
            named = IV[...] == float(u)
            top = jnp.max(jnp.where(named, one, NEG), axis=0, keepdims=True)
            total = jnp.sum(jnp.where(named, jnp.exp2(one - top), 0.0), axis=0, keepdims=True)
            RR[0, h, row, pl.ds(u, 1), :] = top + log2(jnp.maximum(total, 1e-30))

    columns(0, column_logs, first_columns, first_rows)

    def weigh(first, h):
        def body(t, carry):
            for s in range(2):
                p = s * 16 + t
                if first:
                    g = GV[h, pl.ds(ti[s, t], 1), :]
                    W8[h, p] = jnp.exp2(M8[h, p] + (g if s == 0 else g + idle(t)))
                else:
                    W8[h, p] = W8[h, p] * UV[h, pl.ds(ti[s, t], 1), :]
            return carry

        lax.fori_loop(0, 16, body, 0, unroll=16)

    def columns_arrive(it, h):
        take_columns(it, h)
        if it == 0:
            GV[h] = log2(all_mass(tm, h)) - merged(RR[0, h])
        else:
            v = all_mass(tm, h) / jnp.sum(RR[it, h], axis=0)
            UV[h] = v
            GV[h] = GV[h] + log2(v)

    for it in range(1, ITERS):
        for h in range(2):
            columns_arrive(it - 1, h)
            if parts[2]:
                weigh(it == 1, h)
                if h == 0:
                    row_parts()
        for half in range(2):
            if parts[2]:
                row_sums(it, half)
            else:
                give_rows(it, half)

        def rows_arrive(half, it=it):
            take_rows(it, half)
            eight = slice(half * 8, half * 8 + 8)
            for h in range(2):
                u = mass(sm, h, half) / jnp.sum(RC[it, half, :, h], axis=0)
                UV[h, eight] = u
                if it == ITERS - 1:
                    f_out[pl.ds(16 * half + h, 8, stride=2), :] = FV[h, eight] + log2(u)

        def sum_columns(h, it=it):
            one = QS[h]
            for u in range(16):
                named = IV[...] == float(u)
                RR[it, h, row, pl.ds(u, 1), :] = jnp.sum(jnp.where(named, one, 0.0), axis=0, keepdims=True)

        columns(it, column_sums, sum_columns, rows_arrive)

    for h in range(2):
        columns_arrive(ITERS - 1, h)
        g_out[pl.ds(h, 16, stride=2), :] = GV[h]

    if parts[0]:
        for link in range(4):
            quarter = X.at[pl.ds(0, 2), pl.ds(0, 3840)]
            pltpu.make_async_copy(quarter, quarter, gs.at[link]).wait()
    if parts[3] and parts[4]:
        sent = X.at[pl.ds(0, 2), pl.ds(0, 32 * ITERS * (nrow + ncol - 2))]
        pltpu.make_async_copy(sent, sent, es.at[0]).wait()


def build(mesh, parts):
    ncol = mesh.shape["col"]
    nrow = mesh.shape["row"]
    nx = ny = math.isqrt(nrow)

    def on_device(source_points, target_points, source_mass, target_mass, tile_index, tile_count):
        n, d = source_points.shape
        m = target_points.shape[0]
        vmem = pl.BlockSpec(memory_space=pltpu.VMEM)
        hbm = pl.BlockSpec(memory_space=pl.ANY)
        f32 = jnp.float32
        f, g = pl.pallas_call(
            functools.partial(kernel, nx, ny, ncol, parts),
            out_shape=(
                jax.ShapeDtypeStruct((n // 128, 128), f32),
                jax.ShapeDtypeStruct((m // 128, 128), f32),
            ),
            in_specs=[hbm] * 6,
            out_specs=(vmem, vmem),
            scratch_shapes=[
                pltpu.SMEM(tile_index.shape[::-1], jnp.int32),
                pltpu.SMEM(tile_count.shape[::-1], jnp.int32),
                pltpu.VMEM(tile_index.shape[::-1], jnp.int32),
                pltpu.VMEM(tile_count.shape[::-1], jnp.int32),
                pltpu.VMEM((n // 128, 128), f32),
                pltpu.VMEM((m // 128, 128), f32),
                pltpu.VMEM((d // 128, n, 128), jnp.bfloat16),
                *[pltpu.VMEM((m // 128, 256, 128), jnp.bfloat16) for _ in range(4)],
                pltpu.VMEM((2, 32, TILE, 128), f32),
                pltpu.VMEM((32, TILE, TILE), f32),
                pltpu.VMEM((2, 2, TILE, 128), f32),
                pltpu.VMEM((2, 2, TILE, 128), f32),
                pltpu.VMEM((TILE, 128), f32),
                pltpu.VMEM((TILE, 128), f32),
                pltpu.VMEM((16, TILE, 128), f32),
                pltpu.VMEM((2, 32, 128), f32),
                pltpu.VMEM((2, 32, 128), f32),
                pltpu.VMEM((2, 32, 8, 128), f32),
                pltpu.VMEM((2, 32, 8, 128), f32),
                pltpu.VMEM((2, 16, 128), f32),
                pltpu.VMEM((2, 16, 128), f32),
                pltpu.VMEM((2, 16, 128), f32),
                pltpu.VMEM((ITERS, 2, ncol, 2, 8, 128), f32),
                pltpu.VMEM((ITERS, 2, nrow, 16, 128), f32),
                pltpu.VMEM((32, 128), f32),
                pltpu.SemaphoreType.DMA((8,)),
                pltpu.SemaphoreType.DMA((4,)),
                pltpu.SemaphoreType.DMA((30,)),
                pltpu.SemaphoreType.DMA((ITERS, 2)),
                pltpu.SemaphoreType.DMA((ITERS, 2)),
                pltpu.SemaphoreType.DMA((1,)),
            ],
            compiler_params=pltpu.CompilerParams(
                collective_id=0, has_side_effects=True, vmem_limit_bytes=60 * 2**20
            ),
        )(
            tile_index.T, tile_count.T, source_points, target_points.T,
            source_mass.reshape(-1, 128), target_mass.reshape(-1, 128),
        )
        return (f * LN2).reshape(-1), (g * LN2).reshape(-1)

    placed = (P("row", None), P("col", "row"), P("row"), P("col"), P("row", "col"), P("row", "col"))
    return jax.shard_map(
        on_device, mesh=mesh, in_specs=placed, out_specs=(P("row"), P("col")), check_vma=False
    )


def solution(mesh):
    return build(mesh, (True,) * 5)
```

```python
import functools
import math

import jax
import jax.numpy as jnp
from jax import lax
from jax.experimental import pallas as pl
from jax.experimental.pallas import tpu as pltpu
from jax.sharding import PartitionSpec as P

TILE = 256
ITERS = 3
LOG2E = 1.4426950408889634
LN2 = 0.6931471805599453
NEG = -1e30
MESH = pl.DeviceIdType.MESH
HALF = 16
QUART = 8
SHORT = True


def log2(v):
    return jnp.log(v) * LOG2E


def kernel(
    nx, ny, ncol, parts,
    ti_hbm, tc_hbm, sp, tp, sm_hbm, tm_hbm, f_out, g_out,
    ti, tc, tv, cv, sm, tm, X, T0, T1, T2, T3, S, SP, KA, KB, MA, MC, RT, MS, QS, M8, W8, FV, GV, UV, RC, RR, IV,
    lsem, gs, gr, cr, rs, es,
):
    T = (T0, T1, T2, T3)
    row = lax.axis_index("row")
    col = lax.axis_index("col")
    nrow = nx * ny
    x, y = row // ny, lax.rem(row, ny)

    def at(dx, dy):
        return (lax.rem(x + dx + nx, nx) * ny + lax.rem(y + dy + ny, ny), col)

    def hops(d, n):
        return min(d, n - d)

    row_steps = sorted(
        ((dx, dy) for dx in range(nx) for dy in range(ny) if dx or dy),
        key=lambda d: -hops(d[0], nx) - hops(d[1], ny),
    )
    row_peers = [at(*d) for d in row_steps]
    z, core = col // 2, lax.rem(col, 2)
    col_steps = sorted(((dz, dc) for dz in range(ncol // 2) for dc in range(2) if dz or dc), key=lambda d: -hops(d[0], ncol // 2))
    col_peers = [(row, lax.rem(z + dz, ncol // 2) * 2 + lax.rem(core + dc, 2)) for dz, dc in col_steps]

    barrier = pltpu.get_barrier_semaphore()
    greeted = [at(1, 0), at(-1, 0), at(0, 1), at(0, -1)] + col_peers if SHORT else row_peers + col_peers
    for peer in greeted:
        pl.semaphore_signal(barrier, inc=1, device_id=peer, device_id_type=MESH)
    def rows(dy):
        return pl.ds(pl.multiple_of(lax.rem(y + dy + ny, ny) * 64, 64), 64)

    for b in range(32):
        pltpu.make_async_copy(tp.at[:, pl.ds(128 * b, 128)], T[0].at[b, rows(0)], lsem.at[1]).start()

    pl.semaphore_wait(barrier, len(greeted))

    mine = T[0].at[:, rows(0)]
    pltpu.make_async_copy(mine, mine, lsem.at[1]).wait()
    used = []

    steps = {0: (1, 0), 1: (-1, 0), 2: (0, 1), 3: (0, -1)}

    def fresh():
        used.append(0)
        return len(used) - 1

    def send(src, dst, link, k=None):
        k = fresh() if k is None else k
        c = pltpu.make_async_remote_copy(
            src_ref=src, dst_ref=dst, send_sem=gs.at[link], recv_sem=gr.at[k],
            device_id=at(*steps[link]), device_id_type=MESH,
        )
        c.start()
        return c

    A, B = pl.ds(0, HALF), pl.ds(HALF, HALF)
    A0, A1 = pl.ds(0, QUART), pl.ds(QUART, QUART)
    B0, B1 = pl.ds(HALF, QUART), pl.ds(HALF + QUART, QUART)

    def own(part):
        return T[0].at[part, rows(0)]

    def along_y(src, d, part, dy):
        return tuple(send(src, T[d].at[part, rows(dy)], link) for link in (2, 3))

    def along_x(src, part, dy):
        return (
            send(src, T[3].at[part, rows(dy)], 0),
            send(src, T[1].at[part, rows(dy)], 1),
        )

    def forward_y(pair, d, low, high):
        k = fresh()
        pair[0].wait_recv()
        send(T[d].at[low, rows(-1)], T[d].at[low, rows(-1)], 2, k)
        pair[1].wait_recv()
        send(T[d].at[high, rows(1)], T[d].at[high, rows(1)], 3, k)
        return k

    def forward_x(pair, dy, low, high):
        k = fresh()
        pair[0].wait_recv()
        send(T[3].at[low, rows(dy)], T[2].at[low, rows(dy)], 0, k)
        pair[1].wait_recv()
        send(T[1].at[high, rows(dy)], T[2].at[high, rows(dy)], 1, k)
        return k

    def done(*sems):
        for k in sems:
            whole = T[0].at[A, rows(0)]
            pltpu.make_async_copy(whole, whole, gr.at[k]).wait()

    scale = LOG2E / math.sqrt(sp.shape[1])
    wide = (32, 8, 128)

    def fold(op, v):
        v = v.reshape((v.shape[0] // 4, 4) + v.shape[1:])
        v = functools.reduce(op, [v[k] for k in range(v.shape[0])])
        while v.shape[0] > 1:
            n = v.shape[0] // 2
            v = op(v[:n], v[n:])
        return v[0]

    def product(chunks, t, s):
        here = pl.ds(pl.multiple_of(t * TILE, TILE), TILE)
        left = [X[lax.rem(x + d, nx) * 2 + k, here, :] for d in chunks for k in range(2)]
        right = [jnp.concatenate([T[d][ti[s, t] * 2 + k] for k in range(2)], axis=1) for d in chunks]
        return jnp.dot(
            jnp.concatenate(left, axis=1), jnp.concatenate(right, axis=0), preferred_element_type=jnp.float32
        ) * scale

    def scores(*chunks):
        def body(t, carry):
            for s in range(2):
                p = s * 16 + t
                new = product(chunks, t, s)
                SP[p] = new if chunks == (0,) else SP[p] + new
            return carry

        lax.fori_loop(0, 16, body, 0, unroll=2)

    def idle(t):
        return (tc[0, t].astype(jnp.float32) - 2.0) * 1e30

    if parts[0]:
        a1 = along_x(own(A), A, 0)
        b1 = along_y(own(B), 0, B, 0)
        ay0 = along_y(own(A), 0, A, 0)
        bx0 = along_x(own(B), B, 0)

    tables = [
        pltpu.make_async_copy(a, b, lsem.at[2 + k])
        for k, (a, b) in enumerate(
            ((ti_hbm, ti), (tc_hbm, tc), (ti_hbm, tv), (tc_hbm, cv), (sm_hbm, sm), (tm_hbm, tm))
        )
    ]
    for c in tables:
        c.start()
    load_x = [pltpu.make_async_copy(sp.at[:, pl.ds(128 * k, 128)], X.at[k], lsem.at[0]) for k in range(8)]
    for c in load_x:
        c.start()

    for c in tables:
        c.wait()
    small = lax.broadcasted_iota(jnp.int32, (16, 16), 0) == lax.broadcasted_iota(jnp.int32, (16, 16), 1)
    for s in range(2):
        name = jnp.where(cv[...] > s, tv[s:s + 1, :], -1).astype(jnp.float32)
        down = jnp.sum(jnp.where(small, jnp.broadcast_to(name, (16, 16)), 0.0), axis=1, keepdims=True)
        IV[s * 16:(s + 1) * 16, :] = jnp.broadcast_to(down, (16, 128))

    if parts[0]:
        a2 = forward_x(a1, 0, A0, A1)
        ay3 = along_y(T[3].at[A, rows(0)], 3, A, 0)
        ay1 = along_y(T[1].at[A, rows(0)], 1, A, 0)
        b2 = forward_y(b1, 0, B0, B1)
        bx3 = along_x(T[0].at[B, rows(-1)], B, -1)
        bx1 = along_x(T[0].at[B, rows(1)], B, 1)
        fay0 = forward_y(ay0, 0, A0, A1)
        fbx0 = forward_x(bx0, 0, B0, B1)
        done(a2)
        ay2 = along_y(T[2].at[A, rows(0)], 2, A, 0)
        done(b2)
        bx2 = along_x(T[0].at[B, rows(2)], B, 2)
        done(fay0)
    pltpu.make_async_copy(X, X, lsem.at[0]).wait()
    if parts[1]:
        scores(0)
    if parts[0]:
        fay3 = forward_y(ay3, 3, A0, A1)
        fay1 = forward_y(ay1, 1, A0, A1)
        fbx3 = forward_x(bx3, -1, B0, B1)
        fbx1 = forward_x(bx1, 1, B0, B1)
        fay2 = forward_y(ay2, 2, A0, A1)
        fbx2 = forward_x(bx2, 2, B0, B1)
        done(fay3, fay1)
    if parts[1]:
        scores(3, 1)
    if parts[0]:
        done(fbx0, fbx3, fbx1, fay2, fbx2)

    def give(buf, it, part, me, peers, rsem):
        for peer in peers:
            pltpu.make_async_remote_copy(
                src_ref=buf.at[it, part, me], dst_ref=buf.at[it, part, me],
                send_sem=es.at[0], recv_sem=rsem.at[it, part],
                device_id=peer, device_id_type=MESH,
            ).start()

    def take(buf, it, part, n, rsem):
        others = buf.at[it, part, pl.ds(0, n - 1)]
        pltpu.make_async_copy(others, others, rsem.at[it, part]).wait()

    def give_rows(it, half):
        if parts[3]:
            give(RC, it, half, col, col_peers, cr)

    def take_rows(it, half):
        if parts[3]:
            take(RC, it, half, ncol, cr)

    def give_columns(it, h):
        if parts[4]:
            give(RR, it, h, row, row_peers, rs)

    def take_columns(it, h):
        if parts[4]:
            take(RR, it, h, nrow, rs)

    def log_rows(half):
        eight = slice(half * 8, half * 8 + 8)
        for h in range(2):
            RC[0, half, col, h] = MS[h, eight] + log2(QS[h, eight])
        give_rows(0, half)

    def over_lanes(op, v):
        v = fold(op, v.T.reshape(16, 8, 128))
        n = 8
        while n > 1:
            n //= 2
            v = op(v[:n], v[n:])
        return v

    def as_column(v):
        return jnp.broadcast_to(v, (128, 128)).T

    def finish(t, K):
        for s in range(2):
            p = s * 16 + t
            both = SP[p] + product((2,), t, s)
            if s:
                both = both + idle(t)
            for h in range(2):
                S[h, p] = both[:, h * 128:(h + 1) * 128]
                K[s, h] = both[:, h * 128:(h + 1) * 128]

    def lane_logs(K, to):
        r = [K[s, h] for s in range(2) for h in range(2)]
        top = jnp.maximum(jnp.maximum(r[0], r[1]), jnp.maximum(r[2], r[3]))
        e = [jnp.exp2(v - top) for v in r]
        to[...] = top + log2((e[0] + e[1]) + (e[2] + e[3]))

    def row_logs(t, logs):
        for h in range(2):
            v = logs[h * 128:(h + 1) * 128, :].T.reshape(16, 8, 128)
            m8 = fold(jnp.maximum, v)
            s8 = fold(jnp.add, jnp.exp2(v - m8[None]))
            top = jnp.max(m8, axis=0, keepdims=True)
            MS[h, pl.ds(t, 1), :] = top
            QS[h, pl.ds(t, 1), :] = jnp.sum(s8 * jnp.exp2(m8 - top), axis=0, keepdims=True)

    if parts[1]:
        def stages(t, now):
            if 2 in now:
                row_logs(t - 2, MA)
            if 1 in now:
                lane_logs(KA, MA)
            if 0 in now:
                finish(t, KA)

        def step(t, carry):
            stages(t, (2, 1, 0))
            return carry

        stages(0, (0,))
        stages(1, (1, 0))
        lax.fori_loop(2, 10, step, 0)
    log_rows(0)
    if parts[1]:
        lax.fori_loop(10, 16, step, 0)
        stages(16, (2, 1))
        stages(17, (2,))
    log_rows(1)

    def spread(t, to):
        for h in range(2):
            to[h * 128:(h + 1) * 128, :] = as_column(UV[h, pl.ds(t, 1), :])

    def each_tile(visit, half, keep):
        spread(8 * half, MA)

        def body(k, carry):
            t = 8 * half + 2 * k
            spread(t + 1, MC)
            visit(t, MA)
            if keep:
                RT[t] = MA[...]
            spread(lax.min(t + 2, 15), MA)
            visit(t + 1, MC)
            if keep:
                RT[t + 1] = MC[...]
            return carry

        lax.fori_loop(0, 4, body, 0, unroll=2)

    def each_kept(visit):
        def body(k, carry):
            visit(8 + k, RT.at[8 + k])
            return carry

        lax.fori_loop(0, 8, body, 0, unroll=4)

    def block(p, h):
        return S[h, p].reshape(wide)

    def column_logs(t, by, lanes):
        add = by[...].reshape(wide)
        for s in range(2):
            p = s * 16 + t
            for h in lanes:
                c = block(p, h) + add
                m8 = fold(jnp.maximum, c)
                e = jnp.exp2(c - m8[None])
                S[h, p] = e.reshape(TILE, 128)
                M8[h, p] = m8
                s8 = fold(jnp.add, e)
                top = jnp.max(m8, axis=0, keepdims=True)
                MS[h, pl.ds(p, 1), :] = top
                QS[h, pl.ds(p, 1), :] = jnp.sum(s8 * jnp.exp2(m8 - top), axis=0, keepdims=True)

    def row_parts():
        def step(t, carry):
            e = [block(s * 16 + t, 0) * W8[0, s * 16 + t][None] for s in range(2)]
            RT[t] = (e[0] + e[1]).reshape(TILE, 128)
            return carry

        lax.fori_loop(0, 16, step, 0, unroll=2)

    def row_sums(it, half):
        def step(k, carry):
            t = 8 * half + k
            e = [block(s * 16 + t, 1) * W8[1, s * 16 + t][None] for s in range(2)]
            total = RT[t] + (e[0] + e[1]).reshape(TILE, 128)
            for h in range(2):
                RC[it, half, col, h, pl.ds(k, 1), :] = over_lanes(jnp.add, total[h * 128:(h + 1) * 128])
            return carry

        lax.fori_loop(0, 8, step, 0, unroll=8)
        give_rows(it, half)

    def column_sums(t, by, lanes):
        by = by[...].reshape(wide)
        for s in range(2):
            p = s * 16 + t
            for h in lanes:
                s8 = fold(jnp.add, block(p, h) * by) * W8[h, p]
                QS[h, pl.ds(p, 1), :] = jnp.sum(s8, axis=0, keepdims=True)

    def merged(got):
        top = jnp.max(got, axis=0)
        return top + log2(jnp.sum(jnp.exp2(got - top[None]), axis=0))

    def mass(ref, h, half):
        return ref[pl.ds(16 * half + h, 8, stride=2), :]

    def all_mass(ref, h):
        return ref[pl.ds(h, 16, stride=2), :]

    def columns(it, visit, combine, ready):
        ready(0)
        if parts[2]:
            each_tile(functools.partial(visit, lanes=(0, 1)), 0, False)
        ready(1)
        for h in range(2):
            if parts[2] and h == 0:
                each_tile(functools.partial(visit, lanes=(h,)), 1, True)
            elif parts[2]:
                each_kept(functools.partial(visit, lanes=(h,)))
            combine(h)
            give_columns(it, h)

    def first_rows(half):
        take_rows(0, half)
        eight = slice(half * 8, half * 8 + 8)
        for h in range(2):
            f = log2(mass(sm, h, half)) - merged(RC[0, half, :, h])
            FV[h, eight] = f
            UV[h, eight] = f

    def first_columns(h):
        one = MS[h] + log2(QS[h])
        for u in range(16):
            named = IV[...] == float(u)
            top = jnp.max(jnp.where(named, one, NEG), axis=0, keepdims=True)
            total = jnp.sum(jnp.where(named, jnp.exp2(one - top), 0.0), axis=0, keepdims=True)
            RR[0, h, row, pl.ds(u, 1), :] = top + log2(jnp.maximum(total, 1e-30))

    columns(0, column_logs, first_columns, first_rows)

    def weigh(first, h):
        def body(t, carry):
            for s in range(2):
                p = s * 16 + t
                if first:
                    g = GV[h, pl.ds(ti[s, t], 1), :]
                    W8[h, p] = jnp.exp2(M8[h, p] + (g if s == 0 else g + idle(t)))
                else:
                    W8[h, p] = W8[h, p] * UV[h, pl.ds(ti[s, t], 1), :]
            return carry

        lax.fori_loop(0, 16, body, 0, unroll=16)

    def columns_arrive(it, h):
        take_columns(it, h)
        if it == 0:
            GV[h] = log2(all_mass(tm, h)) - merged(RR[0, h])
        else:
            v = all_mass(tm, h) / jnp.sum(RR[it, h], axis=0)
            UV[h] = v
            GV[h] = GV[h] + log2(v)

    for it in range(1, ITERS):
        for h in range(2):
            columns_arrive(it - 1, h)
            if parts[2]:
                weigh(it == 1, h)
                if h == 0:
                    row_parts()
        for half in range(2):
            if parts[2]:
                row_sums(it, half)
            else:
                give_rows(it, half)

        def rows_arrive(half, it=it):
            take_rows(it, half)
            eight = slice(half * 8, half * 8 + 8)
            for h in range(2):
                u = mass(sm, h, half) / jnp.sum(RC[it, half, :, h], axis=0)
                UV[h, eight] = u
                if it == ITERS - 1:
                    f_out[pl.ds(16 * half + h, 8, stride=2), :] = FV[h, eight] + log2(u)

        def sum_columns(h, it=it):
            one = QS[h]
            for u in range(16):
                named = IV[...] == float(u)
                RR[it, h, row, pl.ds(u, 1), :] = jnp.sum(jnp.where(named, one, 0.0), axis=0, keepdims=True)

        columns(it, column_sums, sum_columns, rows_arrive)

    for h in range(2):
        columns_arrive(ITERS - 1, h)
        g_out[pl.ds(h, 16, stride=2), :] = GV[h]

    if parts[0]:
        for link in range(4):
            quarter = X.at[pl.ds(0, 2), pl.ds(0, 3840)]
            pltpu.make_async_copy(quarter, quarter, gs.at[link]).wait()
    if parts[3] and parts[4]:
        sent = X.at[pl.ds(0, 2), pl.ds(0, 32 * ITERS * (nrow + ncol - 2))]
        pltpu.make_async_copy(sent, sent, es.at[0]).wait()


def build(mesh, parts):
    ncol = mesh.shape["col"]
    nrow = mesh.shape["row"]
    nx = ny = math.isqrt(nrow)

    def on_device(source_points, target_points, source_mass, target_mass, tile_index, tile_count):
        n, d = source_points.shape
        m = target_points.shape[0]
        vmem = pl.BlockSpec(memory_space=pltpu.VMEM)
        hbm = pl.BlockSpec(memory_space=pl.ANY)
        f32 = jnp.float32
        f, g = pl.pallas_call(
            functools.partial(kernel, nx, ny, ncol, parts),
            out_shape=(
                jax.ShapeDtypeStruct((n // 128, 128), f32),
                jax.ShapeDtypeStruct((m // 128, 128), f32),
            ),
            in_specs=[hbm] * 6,
            out_specs=(vmem, vmem),
            scratch_shapes=[
                pltpu.SMEM(tile_index.shape[::-1], jnp.int32),
                pltpu.SMEM(tile_count.shape[::-1], jnp.int32),
                pltpu.VMEM(tile_index.shape[::-1], jnp.int32),
                pltpu.VMEM(tile_count.shape[::-1], jnp.int32),
                pltpu.VMEM((n // 128, 128), f32),
                pltpu.VMEM((m // 128, 128), f32),
                pltpu.VMEM((d // 128, n, 128), jnp.bfloat16),
                *[pltpu.VMEM((m // 128, 256, 128), jnp.bfloat16) for _ in range(4)],
                pltpu.VMEM((2, 32, TILE, 128), f32),
                pltpu.VMEM((32, TILE, TILE), f32),
                pltpu.VMEM((2, 2, TILE, 128), f32),
                pltpu.VMEM((2, 2, TILE, 128), f32),
                pltpu.VMEM((TILE, 128), f32),
                pltpu.VMEM((TILE, 128), f32),
                pltpu.VMEM((16, TILE, 128), f32),
                pltpu.VMEM((2, 32, 128), f32),
                pltpu.VMEM((2, 32, 128), f32),
                pltpu.VMEM((2, 32, 8, 128), f32),
                pltpu.VMEM((2, 32, 8, 128), f32),
                pltpu.VMEM((2, 16, 128), f32),
                pltpu.VMEM((2, 16, 128), f32),
                pltpu.VMEM((2, 16, 128), f32),
                pltpu.VMEM((ITERS, 2, ncol, 2, 8, 128), f32),
                pltpu.VMEM((ITERS, 2, nrow, 16, 128), f32),
                pltpu.VMEM((32, 128), f32),
                pltpu.SemaphoreType.DMA((8,)),
                pltpu.SemaphoreType.DMA((4,)),
                pltpu.SemaphoreType.DMA((30,)),
                pltpu.SemaphoreType.DMA((ITERS, 2)),
                pltpu.SemaphoreType.DMA((ITERS, 2)),
                pltpu.SemaphoreType.DMA((1,)),
            ],
            compiler_params=pltpu.CompilerParams(
                collective_id=0, has_side_effects=True, vmem_limit_bytes=60 * 2**20
            ),
        )(
            tile_index.T, tile_count.T, source_points, target_points.T,
            source_mass.reshape(-1, 128), target_mass.reshape(-1, 128),
        )
        return (f * LN2).reshape(-1), (g * LN2).reshape(-1)

    placed = (P("row", None), P("col", "row"), P("row"), P("col"), P("row", "col"), P("row", "col"))
    return jax.shard_map(
        on_device, mesh=mesh, in_specs=placed, out_specs=(P("row"), P("col")), check_vma=False
    )


def solution(mesh):
    return build(mesh, (True,) * 5)
```
